256 devices in a mesh: seq: 64 (over y, z, core), head: 4 (over x).
Axes of the slice: x: 4, y: 4, z: 8, core: 2. Of those that a mesh axis runs over, the one named last changes fastest.
Arguments:
- queries: float32 [8192, 2048], P('seq', 'head'), may hold values from -6 to 6
- keys: float32 [8192, 2048], P('seq', 'head'), may hold values from -6 to 6
- values: float32 [8192, 2048], P('seq', 'head'), may hold values from -6 to 6
- rates: float32 [4, 8192], P('head', 'seq'), may hold values from 0.05 to 1
- gate_fast: float32 [4, 512, 512], P('head'), may hold values from -0.25 to 0.25
- up_fast: float32 [4, 512, 512], P('head'), may hold values from -0.25 to 0.25
- down_fast: float32 [4, 512, 512], P('head'), may hold values from -0.25 to 0.25
- out_proj: bfloat16 [2048, 4096], P('head', 'seq'), may hold values from -0.125 to 0.125
- out_grad: bfloat16 [8192, 4096], P('seq', 'head'), may hold values from -6 to 6
Outputs:
- query_grad: float32 [8192, 2048], P('seq', 'head')
- key_grad: float32 [8192, 2048], P('seq', 'head')
- value_grad: float32 [8192, 2048], P('seq', 'head')
- gate_grad: float32 [4, 512, 512], P('head', 'seq')
- up_grad: float32 [4, 512, 512], P('head', 'seq')
- down_grad: float32 [4, 512, 512], P('head', 'seq')
The draws below stay inside these ranges and needn't reach their ends.
All inputs are finite; a program needn't handle non-finite values.
Results may differ from the reference program's by a relative error of at most 0.0003.
Values may be sent and summed in bfloat16 or wider, within the bound.
A program may use at most 64 MiB of HBM per device.

```python
import math
import jax
import jax.numpy as jnp
from jax import lax

D = 4096
HEAD_DIM = 512
FAST_FF = 512
HEADS = 4
GROUP = 8192


def block_scale(own_key, shape, pieces, low, top_value):
    def one(dim, shards_of):
        heights = jax.random.uniform(jax.random.fold_in(jax.random.fold_in(own_key, 6), dim), (shards_of,), jnp.float32, low / len(pieces), top_value / len(pieces))
        return jnp.repeat(jnp.exp(heights), shape[dim] // shards_of).reshape((-1,) + (1,) * (len(shape) - dim - 1))

    gain = one(*pieces[0])
    for cut in pieces[1:]:
        gain = gain * one(*cut)
    return gain


def noise(rng, shape, width, limit, split=(), held_as=jnp.bfloat16):
    values = width * jax.random.normal(rng, shape, jnp.float32)
    if split:
        values = values * block_scale(rng, shape, split, -0.22, 0.18)
    return jnp.clip(values, -limit, limit).astype(held_as)


def setup_inputs(seed: int = 0) -> dict:
    seeds = jax.random.split(jax.random.key(seed), 10)
    return {
        "queries": noise(seeds[0], (GROUP, HEADS * HEAD_DIM), 1.0, 6.0, ((0, 64), (1, 4)), jnp.float32),
        "keys": noise(seeds[1], (GROUP, HEADS * HEAD_DIM), 1.0, 6.0, ((0, 64), (1, 4)), jnp.float32),
        "values": noise(seeds[2], (GROUP, HEADS * HEAD_DIM), 1.0, 6.0, ((0, 64), (1, 4)), jnp.float32),
        "rates": jnp.clip(jnp.exp(math.log(1.0) - 2.9957323 * jax.random.uniform(seeds[3], (HEADS, GROUP), jnp.float32) ** block_scale(seeds[3], (HEADS, GROUP), ((0, 4), (1, 64)), -0.2, 0.2)), 0.05, 1.0),
        "gate_fast": noise(seeds[4], (HEADS, FAST_FF, HEAD_DIM), HEAD_DIM ** -0.5, 0.25, ((0, 4),), jnp.float32),
        "up_fast": noise(seeds[5], (HEADS, FAST_FF, HEAD_DIM), HEAD_DIM ** -0.5, 0.25, ((0, 4),), jnp.float32),
        "down_fast": noise(seeds[6], (HEADS, HEAD_DIM, FAST_FF), FAST_FF ** -0.5, 0.25, ((0, 4),), jnp.float32),
        "out_proj": noise(seeds[7], (HEADS * HEAD_DIM, D), (HEADS * HEAD_DIM) ** -0.5, 0.125, ((0, 4), (1, 64))),
        "out_grad": noise(seeds[8], (GROUP, D), 1.0, 6.0, ((0, 64), (1, 4))),
    }


def matmul(left, right):
    return jnp.dot(left, right, precision=lax.Precision.HIGHEST, preferred_element_type=jnp.float32)

def swiglu(gate_matrix, up_matrix, down_matrix, inputs):
    before = matmul(inputs, gate_matrix.T)
    linear = matmul(inputs, up_matrix.T)
    hidden = jax.nn.silu(before) * linear
    return matmul(hidden, down_matrix.T)

def update_terms(gate_matrix, up_matrix, down_matrix, key_rows, value_rows, rate_rows):
    before = matmul(key_rows, gate_matrix.T)
    linear = matmul(key_rows, up_matrix.T)
    sigma = jax.nn.sigmoid(before)
    activated = before * sigma
    hidden = activated * linear
    target = -(rate_rows[:, None] * value_rows)
    term_down = matmul(target.T, hidden)
    hidden_grad = matmul(target, down_matrix)
    before_grad = hidden_grad * linear * sigma * (1.0 + before * (1.0 - sigma))
    linear_grad = hidden_grad * activated
    return (matmul(before_grad.T, key_rows), matmul(linear_grad.T, key_rows), term_down)

def renorm(weight, partial_value, total_sq, scale):
    norm_update = jnp.sqrt(total_sq + 1e-06)
    moved = weight - partial_value * (scale / norm_update)[..., None, None]
    norm_old = jnp.sqrt(lax.optimization_barrier(jnp.sum(weight * weight, axis=-1)) + 1e-06)
    norm_new = jnp.sqrt(lax.optimization_barrier(jnp.sum(moved * moved, axis=-1)) + 1e-06)
    return (moved * (norm_old / norm_new)[..., None], norm_new, norm_update)

def back_rows(weight, renormed, norm_new, grad, norm_update, scale):
    norm_old = jnp.sqrt(lax.optimization_barrier(jnp.sum(weight * weight, axis=-1)) + 1e-06)
    moved = renormed * (norm_new / norm_old)[..., None]
    partial_value = (weight - moved) * (norm_update / scale)[..., None, None]
    along = lax.optimization_barrier(jnp.sum(moved * grad, axis=-1))
    moved_grad = (norm_old / norm_new)[..., None] * (grad - moved * (along / (norm_new * norm_new))[..., None])
    direct = moved_grad + (along / (norm_new * norm_old))[..., None] * weight
    return (direct, -moved_grad, partial_value)

def step_back(step_grad, partial_value, inner, norm_update, scale):
    factor = inner / (norm_update * norm_update)
    return (scale / norm_update)[..., None, None] * (step_grad - partial_value * factor[..., None, None])

def reference(queries, keys, values, rates, gate_fast, up_fast, down_fast, out_proj, out_grad):
    head_size = gate_fast.shape[2]
    out_cot = jnp.dot(out_grad, out_proj.T, preferred_element_type=jnp.float32)
    query_list, key_list, value_list = ([], [], [])
    gate_list, up_list, down_list = ([], [], [])
    for member in range(gate_fast.shape[0]):
        lower = member * head_size
        upper = lower + head_size
        weights = (gate_fast[member], up_fast[member], down_fast[member])
        scales = tuple((0.3 * math.sqrt(matrix.shape[0]) for matrix in weights))
        rate_rows = rates[member]

        def update_of(gate_matrix, up_matrix, down_matrix, key_rows, value_rows):
            return update_terms(gate_matrix, up_matrix, down_matrix, key_rows, value_rows, rate_rows)
        partials, update_pull = jax.vjp(update_of, weights[0], weights[1], weights[2], keys[:, lower:upper], values[:, lower:upper])
        normed = [renorm(weights[slot], partials[slot], jnp.sum(partials[slot] * partials[slot]), scales[slot]) for slot in range(3)]
        applied, apply_pull = jax.vjp(swiglu, normed[0][0], normed[1][0], normed[2][0], queries[:, lower:upper])
        cot_gate, cot_up, cot_down, query_part = apply_pull(out_cot[:, lower:upper])
        cots = (cot_gate, cot_up, cot_down)
        directs, directions = ([], [])
        for slot in range(3):
            direct, step_grad, partial_value = back_rows(weights[slot], normed[slot][0], normed[slot][1], cots[slot], normed[slot][2], scales[slot])
            inner = jnp.sum(partial_value * step_grad)
            directs.append(direct)
            directions.append(step_back(step_grad, partial_value, inner, normed[slot][2], scales[slot]))
        through_gate, through_up, through_down, key_part, value_part = update_pull((directions[0], directions[1], directions[2]))
        query_list.append(query_part)
        key_list.append(key_part)
        value_list.append(value_part)
        gate_list.append(directs[0] + through_gate)
        up_list.append(directs[1] + through_up)
        down_list.append(directs[2] + through_down)
    return (jnp.concatenate(query_list, axis=1), jnp.concatenate(key_list, axis=1), jnp.concatenate(value_list, axis=1), jnp.stack(gate_list), jnp.stack(up_list), jnp.stack(down_list))
```

```python
import math

import jax
import jax.numpy as jnp
from jax import lax
from jax.experimental import pallas as pl
from jax.experimental.pallas import tpu as pltpu
from jax.sharding import Mesh
from jax.sharding import PartitionSpec as P

MESH = pl.DeviceIdType.MESH
SEQ = ("y", "z", "c")
F32 = jnp.float32
BF16 = jnp.bfloat16
NY, NZ, NC, NX = 4, 8, 2, 4
TOK = 128
D = 512
FS = 64
SCALE = 0.3 * math.sqrt(512)
EPS = 1e-06


def halves(x):
    hi = x.astype(BF16)
    return hi, (x - hi.astype(F32)).astype(BF16)


def dot_nt(a, b):
    return lax.dot_general(a, b, (((1,), (1,)), ((), ())), preferred_element_type=F32)


def dot_nn(a, b):
    return lax.dot_general(a, b, (((1,), (0,)), ((), ())), preferred_element_type=F32)


def dot_tn(a, b):
    return lax.dot_general(a, b, (((0,), (0,)), ((), ())), preferred_element_type=F32)


def three(product, a, b_hi, b_lo):
    hi, lo = halves(a)
    n = a.shape[0]
    both = product(jnp.concatenate([hi, lo], axis=0), b_hi)
    return both[:n] + both[n:] + product(hi, b_lo)


def back(acts, mats):
    a_hi, a_lo = halves(acts)
    m_hi, m_lo = halves(mats)
    return dot_tn(
        jnp.concatenate([a_hi, a_lo, a_hi], axis=0), jnp.concatenate([m_hi, m_hi, m_lo], axis=0)
    )


def row_sum(x):
    return jnp.sum(x, axis=1, keepdims=True)


def col_sum(x):
    return jnp.sum(x, axis=0, keepdims=True)


def total(x):
    return jnp.sum(jnp.sum(x, axis=1, keepdims=True), axis=0, keepdims=True)


def kernel(
    q_ref, k_ref, v_ref, rate_ref, g_hbm, u_hbm, w_hbm, oproj_ref, ograd_ref,
    qg_ref, kg_ref, vg_ref, gg_ref, ug_ref, dg_ref,
    k2, t2, q2, o2, oproj_sib, ochunk, oall, grads,
    gs, us, wcol, wts,
    before_s, linear_s, hgrad_s,
    s1, r1, a1, st1, sty1, sts1, stz1,
    s2, r2, a2, st2, sty2, sts2, stz2,
    s3, r3, d3, rd3, ds3, dr3,
    part_q, sib_q, sum_q, rec_q, part_k, sib_k, sum_k, rec_k, part_t, sib_t, sum_t, rec_t,
    sems, lsem,
):
    y, z, c, x = (lax.axis_index(name) for name in ("y", "z", "c", "head"))
    used = [0]

    def at_y(dy, other=False):
        return (lax.rem(y + dy, NY), z, 1 - c if other else c, x)

    def at_z(dz):
        return (y, lax.rem(z + dz, NZ), c, x)

    def at_x(dx):
        return (y, z, c, lax.rem(x + dx, NX))

    sibling = (y, z, 1 - c, x)
    y_order = (1, 3, 2)
    z_order = (4, 3, 5, 2, 6, 1, 7)

    def send(src, dst, device):
        i = used[0]
        used[0] += 2
        copy = pltpu.make_async_remote_copy(
            src_ref=src, dst_ref=dst, send_sem=sems.at[i], recv_sem=sems.at[i + 1],
            device_id=device, device_id_type=MESH,
        )
        copy.start()
        started.append(copy)
        return copy

    started = []

    def arrived(copies):
        for copy in copies:
            copy.wait_recv()

    loads = []
    for i, (src, dst) in enumerate(
        (
            (g_hbm.at[y, :, c], gs),
            (u_hbm.at[y, :, c], us),
            (w_hbm.at[:, pl.ds(pl.multiple_of(y * 128, 128), 128)], wcol),
        )
    ):
        copy = pltpu.make_async_copy(src, dst, lsem.at[i])
        copy.start()
        loads.append(copy)

    barrier = pltpu.get_barrier_semaphore()
    partners = [sibling]
    partners += [at_y(d) for d in (1, 2, 3)] + [at_y(d, True) for d in (1, 2, 3)]
    partners += [at_z(d) for d in range(1, NZ)] + [at_x(d) for d in (1, 2, 3)]
    for device in partners:
        pl.semaphore_signal(barrier, inc=1, device_id=device, device_id_type=MESH)
    pl.semaphore_wait(barrier, len(partners))

    me = 2 * y + c

    osib = send(
        oproj_ref.at[pl.ds(pl.multiple_of((1 - c) * 256, 256), 256)], oproj_sib, sibling
    )
    tokens = pl.ds(pl.multiple_of(c * TOK, TOK), TOK)
    grads[x, tokens, :] = ograd_ref[...]
    xs = [send(grads.at[x, tokens], grads.at[x, tokens], at_x(d)) for d in (1, 3, 2)]
    gsib = [send(grads.at[x, tokens], grads.at[x, tokens], sibling)]

    def place(buffer, value):
        hi, lo = halves(value)
        buffer[me, 0] = hi
        buffer[me, 1] = lo

    def to_y(buffer):
        return [send(buffer.at[me], buffer.at[me], at_y(d)) for d in y_order]

    def forward(buffer, copies):
        result = []
        for d, copy in zip(y_order, copies):
            copy.wait_recv()
            block = 2 * lax.rem(y + NY - d, NY) + c
            result.append(send(buffer.at[block], buffer.at[block], sibling))
        return result

    place(k2, k_ref[...])
    ky = to_y(k2)
    rate_cols = jnp.broadcast_to(rate_ref[...], (TOK, TOK)).T
    rate_full = jnp.concatenate([rate_cols] * 4, axis=1)
    place(t2, -(rate_full * v_ref[...]))
    ty = to_y(t2)
    ksib = [send(k2.at[me], k2.at[me], sibling)]
    tsib = [send(t2.at[me], t2.at[me], sibling)]

    osib.wait_recv()
    own = oproj_ref[pl.ds(pl.multiple_of(c * 256, 256), 256), :].astype(F32)
    other = oproj_sib[...].astype(F32)
    first = c == 0
    ochunk[...] = jnp.concatenate(
        [jnp.where(first, own, other), jnp.where(first, other, own)], axis=1
    ).astype(BF16)
    zcols = pl.ds(pl.multiple_of(z * 128, 128), 128)
    oall[y, :, zcols] = ochunk[...]
    oz = [send(ochunk, oall.at[y, :, zcols], at_z(d)) for d in z_order]

    place(q2, q_ref[...])
    for copy in loads:
        copy.wait()
    wt = wcol[...].T.reshape(NZ, 2, 8, D)
    wts[...] = jnp.where(first, wt[:, 0], wt[:, 1])

    ksib += forward(k2, ky)
    tsib += forward(t2, ty)

    arrived(oz)
    oy = [send(oall.at[y], oall.at[y], at_y(d)) for d in y_order]
    arrived(ksib)
    arrived(tsib)

    def flat(ref):
        return ref[...].reshape(FS, D)

    def whole(buffer):
        return tuple(buffer[:, i].reshape(8 * TOK, D) for i in (0, 1))

    def silu_parts(before):
        sigma = jax.nn.sigmoid(before)
        return sigma, before * sigma, sigma * (1.0 + before * (1.0 - sigma))

    with jax.named_scope("partials"):
        both = three(dot_nt, jnp.concatenate([flat(gs), flat(us)], axis=0), *whole(k2))
        before, linear = both[:FS], both[FS:]
        hgrad = three(dot_nt, flat(wts), *whole(t2))
        before_s[...] = before
        linear_s[...] = linear
        hgrad_s[...] = hgrad
        sigma, act, dsilu = silu_parts(before)
        pgu = three(
            dot_nn, jnp.concatenate([hgrad * linear * dsilu, hgrad * act], axis=0), *whole(k2)
        )
        pd = three(dot_nn, act * linear, *whole(t2))
        s1[:, 0:8] = pgu[:FS].reshape(NZ, 8, D)
        s1[:, 8:16] = pgu[FS:].reshape(NZ, 8, D)
        s1[:, 16:24] = pd.reshape(NZ, 8, D)

    def scatter_z(src, dst):
        return [
            send(src.at[lax.rem(z + d, NZ)], dst.at[z], at_z(d)) for d in z_order
        ]

    def gather_z(buffer):
        return [send(buffer.at[z], buffer.at[z], at_z(d)) for d in z_order]

    def summed_z(src, dst, copies):
        value = src[z]
        for d, copy in zip(z_order, copies):
            copy.wait_recv()
            value = value + dst[lax.rem(z + NZ - d, NZ)]
        return value

    def plane_sum(st, sty, sts, stz, value):
        st[...] = value
        sends = [send(st, sty.at[me], sibling)]
        sends += [send(st, sty.at[me], at_y(d)) for d in (1, 2, 3)]
        sends += [send(st, sty.at[me], at_y(d, True)) for d in (1, 2, 3)]
        sty[me] = value
        arrived(sends)
        group = jnp.sum(sty[...], axis=0)
        sts[...] = group
        stz[z] = group
        sends = [send(sts, stz.at[z], at_z(d)) for d in z_order]
        return sends

    rs1 = scatter_z(s1, r1)

    for d, copy in zip((1, 3, 2), xs):
        copy.wait_recv()
        src = lax.rem(x + NX - d, NX)
        gsib.append(send(grads.at[src, tokens], grads.at[src, tokens], sibling))

    chunk = summed_z(s1, r1, rs1)
    a1[z] = chunk
    ag1 = gather_z(a1)
    gc, uc, wc = gs[z], us[z], wts[z]
    pg_c, pu_c, pd_c = chunk[0:8], chunk[8:16], chunk[16:24]
    zs1 = plane_sum(
        st1, sty1, sts1, stz1,
        jnp.concatenate(
            [
                col_sum(pg_c * pg_c), col_sum(pu_c * pu_c), col_sum(pd_c * pd_c),
                col_sum(wc * pd_c), col_sum(wc * wc), jnp.zeros((3, D), F32),
            ],
            axis=0,
        ),
    )
    qy = to_y(q2)
    qsib = [send(q2.at[me], q2.at[me], sibling)]

    arrived(gsib)
    arrived(oy)
    cot = dot_nt(grads[0], oall[0])
    for i in (1, 2, 3):
        cot = cot + dot_nt(grads[i], oall[i])
    cot_hi, cot_lo = halves(cot)
    cols = pl.ds(pl.multiple_of(c * 256, 256), 256)
    rows = pl.ds(2 * y, 2)
    o2[rows, 0, :, cols] = cot_hi.reshape(2, TOK, 256)
    o2[rows, 1, :, cols] = cot_lo.reshape(2, TOK, 256)
    here = o2.at[rows, :, :, cols]
    coty = [send(here, here, at_y(d)) for d in y_order]
    cotsib = [send(here, here, sibling)]

    qsib += forward(q2, qy)
    for d, copy in zip(y_order, coty):
        copy.wait_recv()
        there = o2.at[pl.ds(2 * lax.rem(y + NY - d, NY), 2), :, :, cols]
        cotsib.append(send(there, there, sibling))

    arrived(zs1)
    arrived(ag1)

    with jax.named_scope("renormed"):
        stats = jnp.sum(stz1[...], axis=0)
        pn_g = jnp.sqrt(total(stats[0:1]) + EPS)
        pn_u = jnp.sqrt(total(stats[1:2]) + EPS)
        pn_d = jnp.sqrt(total(stats[2:3]) + EPS)
        k_g, k_u, k_d = SCALE / pn_g, SCALE / pn_u, SCALE / pn_d
        d_pp, d_wp, d_ww = stats[2:3], stats[3:4], stats[4:5]
        old_d = jnp.sqrt(d_ww + EPS)
        new_d = jnp.sqrt(
            jnp.maximum(d_ww - 2.0 * k_d * d_wp + k_d * k_d * d_pp, 0.0) + EPS
        )
        d_pm = d_wp - k_d * d_pp

        def moved_rows(matrix, partial, k):
            moved = matrix - partial * k
            old = jnp.sqrt(row_sum(matrix * matrix) + EPS)
            new = jnp.sqrt(row_sum(moved * moved) + EPS)
            return moved, old, new

        g_m, u_m, w_m = flat(gs), flat(us), flat(wts)
        p_g = a1[:, 0:8].reshape(FS, D)
        p_u = a1[:, 8:16].reshape(FS, D)
        p_d = a1[:, 16:24].reshape(FS, D)
        mv_g, old_g, new_g = moved_rows(g_m, p_g, k_g)
        mv_u, old_u, new_u = moved_rows(u_m, p_u, k_u)
        mv_d = w_m - p_d * k_d
        ren_gu = jnp.concatenate([mv_g * (old_g / new_g), mv_u * (old_u / new_u)], axis=0)
        ren_d = mv_d * (old_d / new_d)

    arrived(qsib)
    arrived(cotsib)
    with jax.named_scope("cotangents"):
        both = three(dot_nt, ren_gu, *whole(q2))
        before, linear = both[:FS], both[FS:]
        hcot = three(dot_nt, ren_d, *whole(o2))
        sigma, act, dsilu = silu_parts(before)
        acts_q = jnp.concatenate([hcot * linear * dsilu, hcot * act], axis=0)
        cgu = three(dot_nn, acts_q, *whole(q2))
        cd = three(dot_nn, act * linear, *whole(o2))
        s2[:, 0:8] = cgu[:FS].reshape(NZ, 8, D)
        s2[:, 8:16] = cgu[FS:].reshape(NZ, 8, D)
        s2[:, 16:24] = cd.reshape(NZ, 8, D)
    rs2 = scatter_z(s2, r2)
    with jax.named_scope("query_grad"):
        part_q[...] = back(acts_q, ren_gu).reshape(NY, 2, TOK, D)
    sibq = send(part_q.at[:, 1 - c], sib_q, sibling)

    chunk2 = summed_z(s2, r2, rs2)
    a2[z] = chunk2
    ag2 = gather_z(a2)

    def row_back(matrix, partial, k, grad):
        moved, old, new = moved_rows(matrix, partial, k)
        along = row_sum(moved * grad)
        moved_grad = (old / new) * (grad - moved * (along / (new * new)))
        return moved_grad, moved_grad + (along / (new * old)) * matrix

    cg_c, cu_c, cd_c = chunk2[0:8], chunk2[8:16], chunk2[16:24]
    mg_c, direct_g = row_back(gc, pg_c, k_g, cg_c)
    mu_c, direct_u = row_back(uc, pu_c, k_u, cu_c)
    zs2 = plane_sum(
        st2, sty2, sts2, stz2,
        jnp.concatenate(
            [
                -col_sum(pg_c * mg_c), -col_sum(pu_c * mu_c),
                col_sum((wc - pd_c * k_d) * cd_c), col_sum(pd_c * cd_c),
                jnp.zeros((4, D), F32),
            ],
            axis=0,
        ),
    )

    def to_owner(part, sib, summed, rec, copy):
        copy.wait_recv()
        summed[...] = part[:, c] + sib[...]
        return [
            send(summed.at[lax.rem(y + d, NY)], rec.at[y], at_y(d)) for d in y_order
        ]

    def owned(summed, rec, copies):
        value = summed[y]
        for d, copy in zip(y_order, copies):
            copy.wait_recv()
            value = value + rec[lax.rem(y + NY - d, NY)]
        return value

    yq = to_owner(part_q, sib_q, sum_q, rec_q, sibq)

    arrived(zs2)
    arrived(ag2)
    with jax.named_scope("direction"):
        stats2 = jnp.sum(stz2[...], axis=0)
        inner_g, inner_u = total(stats2[0:1]), total(stats2[1:2])
        along_d, d_pg = stats2[2:3], stats2[3:4]
        ratio_d = old_d / new_d
        shrink_d = along_d / (new_d * new_d)
        inner_d = -total(ratio_d * (d_pg - d_pm * shrink_d))
        c_g = a2[:, 0:8].reshape(FS, D)
        c_u = a2[:, 8:16].reshape(FS, D)
        c_d = a2[:, 16:24].reshape(FS, D)
        mgrad_g, _ = row_back(g_m, p_g, k_g, c_g)
        mgrad_u, _ = row_back(u_m, p_u, k_u, c_u)
        mgrad_d = ratio_d * (c_d - mv_d * shrink_d)
        direct_d = mgrad_d + (along_d / (new_d * old_d)) * w_m
        dir_g = -k_g * (mgrad_g + p_g * (inner_g / (pn_g * pn_g)))
        dir_u = -k_u * (mgrad_u + p_u * (inner_u / (pn_u * pn_u)))
        dir_d = -k_d * (mgrad_d + p_d * (inner_d / (pn_d * pn_d)))

    with jax.named_scope("through"):
        both = three(dot_nt, jnp.concatenate([dir_g, dir_u], axis=0), *whole(k2))
        d_bg, d_lg = both[:FS], both[FS:]
        d_hid = three(dot_nt, dir_d, *whole(t2))
        before, linear, hgrad = before_s[...], linear_s[...], hgrad_s[...]
        sigma, act, dsilu = silu_parts(before)
        curve = sigma * (1.0 - sigma) * (2.0 + before * (1.0 - 2.0 * sigma))
        d_h = d_bg * linear * dsilu + d_lg * act
        d_l = d_bg * hgrad * dsilu + d_hid * act
        d_b = d_bg * hgrad * linear * curve + (d_lg * hgrad + d_hid * linear) * dsilu
        part_t[...] = back(
            jnp.concatenate([act * linear, d_h], axis=0),
            jnp.concatenate([dir_d, w_m], axis=0),
        ).reshape(NY, 2, TOK, D)
        sibt = send(part_t.at[:, 1 - c], sib_t, sibling)
        part_k[...] = back(
            jnp.concatenate([hgrad * linear * dsilu, hgrad * act, d_b, d_l], axis=0),
            jnp.concatenate([dir_g, dir_u, g_m, u_m], axis=0),
        ).reshape(NY, 2, TOK, D)
        sibk = send(part_k.at[:, 1 - c], sib_k, sibling)
        yt = to_owner(part_t, sib_t, sum_t, rec_t, sibt)
        th_d = three(dot_nn, d_h, *whole(t2))
        th_d = th_d + jnp.where(z == 0, direct_d, jnp.zeros_like(direct_d))
        th_d = th_d.reshape(NZ, 1, 8, D)
        none = jnp.zeros_like(th_d)
        th_d = jnp.concatenate(
            [jnp.where(first, th_d, none), jnp.where(first, none, th_d)], axis=1
        ).reshape(2 * FS, D)
        th_t = th_d.T.reshape(NY, NZ, 2, 8, 2 * FS)
        for i in range(NZ):
            d3[i] = th_t[:, i].reshape(8, 8, 2 * FS)
        rsd = scatter_z(d3, rd3)
        yk = to_owner(part_k, sib_k, sum_k, rec_k, sibk)
        th_gu = three(dot_nn, jnp.concatenate([d_b, d_l], axis=0), *whole(k2))
        s3[:, 0:8] = th_gu[:FS].reshape(NZ, 8, D)
        s3[:, 8:16] = th_gu[FS:].reshape(NZ, 8, D)
        rs3 = scatter_z(s3, r3)

    qg_ref[...] = owned(sum_q, rec_q, yq)
    down = summed_z(d3, rd3, rsd)
    ds3[...] = down
    dr3[me] = ds3[me]
    fin = [send(ds3.at[2 * y + 1 - c], dr3.at[me], sibling)]
    for d in (1, 2, 3):
        to = 2 * lax.rem(y + d, NY)
        fin.append(send(ds3.at[to + c], dr3.at[me], at_y(d)))
        fin.append(send(ds3.at[to + 1 - c], dr3.at[me], at_y(d, True)))
    vg_ref[...] = -(rate_full * owned(sum_t, rec_t, yt))
    kg_ref[...] = owned(sum_k, rec_k, yk)
    gate_up = summed_z(s3, r3, rs3)
    gg_ref[...] = gate_up[0:8] + direct_g
    ug_ref[...] = gate_up[8:16] + direct_u
    arrived(fin)
    dg_ref[...] = jnp.concatenate(
        [dr3[2 * i] + dr3[2 * i + 1] for i in range(NY)], axis=1
    )
    for copy in started:
        copy.wait_send()


def body(queries, keys, values, rates, gate_fast, up_fast, down_fast, out_proj, out_grad):
    vmem = pl.BlockSpec(memory_space=pltpu.VMEM)
    hbm = pl.BlockSpec(memory_space=pl.ANY)

    def buf(*shape, dtype=F32):
        return pltpu.VMEM(shape, dtype)

    exchange = [buf(NZ, 24, D)] * 3 + [buf(8, D), buf(8, 8, D), buf(8, D), buf(NZ, 8, D)]
    grads = [buf(NY, 2, TOK, D), buf(NY, TOK, D), buf(NY, TOK, D), buf(NY, TOK, D)]
    outs = pl.pallas_call(
        kernel,
        out_shape=[jax.ShapeDtypeStruct((TOK, D), F32)] * 3
        + [jax.ShapeDtypeStruct((8, D), F32)] * 3,
        in_specs=[vmem] * 4 + [hbm] * 3 + [vmem] * 2,
        out_specs=[vmem] * 6,
        scratch_shapes=[buf(8, 2, TOK, D, dtype=BF16)] * 4
        + [
            buf(256, 64, dtype=BF16),
            buf(256, 128, dtype=BF16),
            buf(NY, 256, 1024, dtype=BF16),
            buf(NX, 256, 1024, dtype=BF16),
            buf(NZ, 8, D), buf(NZ, 8, D), buf(D, 128), buf(NZ, 8, D),
        ]
        + [buf(FS, 8 * TOK)] * 3
        + exchange
        + exchange
        + [
            buf(NZ, 16, D), buf(NZ, 16, D),
            buf(NZ, 8, 8, 128), buf(NZ, 8, 8, 128), buf(8, 8, 128), buf(8, 8, 128),
        ]
        + grads * 3
        + [pltpu.SemaphoreType.DMA((320,)), pltpu.SemaphoreType.DMA((3,))],
        compiler_params=pltpu.CompilerParams(
            collective_id=0, has_side_effects=True, vmem_limit_bytes=58 * 2**20
        ),
    )(
        queries, keys, values, rates,
        gate_fast.reshape(NY, NZ, 2, 8, D), up_fast.reshape(NY, NZ, 2, 8, D),
        down_fast.reshape(D, D), out_proj, out_grad,
    )
    return (*outs[:3], *(o.reshape(1, 8, D) for o in outs[3:]))


def solution(mesh):
    torus = Mesh(mesh.devices.reshape(NY, NZ, NC, NX), ("y", "z", "c", "head"))
    return jax.shard_map(
        body,
        mesh=torus,
        in_specs=(
            P(SEQ, "head"), P(SEQ, "head"), P(SEQ, "head"), P("head", SEQ),
            P("head", None, None), P("head", None, None), P("head", None, None),
            P("head", SEQ), P(SEQ, "head"),
        ),
        out_specs=(
            P(SEQ, "head"), P(SEQ, "head"), P(SEQ, "head"),
            P("head", SEQ, None), P("head", SEQ, None), P("head", SEQ, None),
        ),
        check_vma=False,
    )
```

```python
import math

import jax
import jax.numpy as jnp
from jax import lax
from jax.experimental import pallas as pl
from jax.experimental.pallas import tpu as pltpu
from jax.sharding import Mesh
from jax.sharding import PartitionSpec as P

MESH = pl.DeviceIdType.MESH
SEQ = ("y", "z", "c")
F32 = jnp.float32
BF16 = jnp.bfloat16
NY, NZ, NC, NX = 4, 8, 2, 4
TOK = 128
D = 512
FS = 64
SCALE = 0.3 * math.sqrt(512)
EPS = 1e-06
SPAN = 251.0
LOW = 125.0


def halves(x):
    hi = x.astype(BF16)
    return hi, (x - hi.astype(F32)).astype(BF16)


def dot_nt(a, b):
    return lax.dot_general(a, b, (((1,), (1,)), ((), ())), preferred_element_type=F32)


def dot_nn(a, b):
    return lax.dot_general(a, b, (((1,), (0,)), ((), ())), preferred_element_type=F32)


def dot_tn(a, b):
    return lax.dot_general(a, b, (((0,), (0,)), ((), ())), preferred_element_type=F32)


def three(product, a, b_hi, b_lo):
    hi, lo = halves(a)
    n = a.shape[0]
    both = product(jnp.concatenate([hi, lo], axis=0), b_hi)
    return both[:n] + both[n:] + product(hi, b_lo)


def back(acts, mats):
    a_hi, a_lo = halves(acts)
    m_hi, m_lo = halves(mats)
    return dot_tn(
        jnp.concatenate([a_hi, a_lo, a_hi], axis=0), jnp.concatenate([m_hi, m_hi, m_lo], axis=0)
    )


def encode(x, top):
    size = jnp.exp2(jnp.abs(x) * (SPAN / top) - LOW)
    return jnp.where(x < 0, -size, size).astype(BF16)


def decode(codes):
    value = codes.astype(F32)
    size = jnp.log2(jnp.abs(value)) + LOW
    return jnp.where(value < 0, -size, size)


def row_top(x):
    return jnp.maximum(jnp.max(jnp.abs(x), axis=-1, keepdims=True), 1e-30)


def as_row(column):
    return jnp.broadcast_to(column, (TOK, TOK)).T[0:1]


def as_columns(row, tiles):
    return jnp.concatenate([jnp.broadcast_to(row, (TOK, TOK)).T] * tiles, axis=1)


def pack(gate, up, down):
    wide = jnp.concatenate([gate, up], axis=1)
    thin = jnp.concatenate([down[..., :256], down[..., 256:]], axis=1)
    top_w = (row_top(wide) * 1.01).astype(BF16)
    top_t = (row_top(thin) * 1.01).astype(BF16)
    top_w32, top_t32 = top_w.astype(F32), top_t.astype(F32)
    lanes = (*wide.shape[:2], 64)
    tops = jnp.concatenate(
        [jnp.broadcast_to(top_w32, lanes), jnp.broadcast_to(top_t32, lanes)], axis=2
    ).astype(BF16)
    return encode(wide, top_w32), encode(thin, top_t32), tops


def unpack(codes):
    tops = codes[..., 768:896].astype(F32) * (1.0 / SPAN)
    wide = decode(codes[..., :512]) * tops[..., 0:1]
    thin = decode(codes[..., 512:768]) * tops[..., 64:65]
    down = jnp.concatenate([thin[:, :8], thin[:, 8:]], axis=2)
    return wide[:, :8], wide[:, 8:], down


def row_sum(x):
    return jnp.sum(x, axis=1, keepdims=True)


def col_sum(x):
    return jnp.sum(x, axis=0, keepdims=True)


def total(x):
    return jnp.sum(jnp.sum(x, axis=1, keepdims=True), axis=0, keepdims=True)


def kernel(
    q_ref, k_ref, v_ref, rate_ref, g_hbm, u_hbm, w_hbm, oproj_ref, ograd_ref,
    qg_ref, kg_ref, vg_ref, gg_ref, ug_ref, dg_ref,
    k2, t2, q2, o2, kc, tc, qc, oc, tops_s, tops, otops, oproj_sib, oall, grads,
    gs, us, wcol, wts,
    before_s, linear_s, hgrad_s,
    s1, c1, r1, a1, st1, sty1, sts1, stz1,
    s2, c2, r2, a2, st2, sty2, sts2, stz2,
    s3, c3, r3, d3, rd3, ds3, dr3,
    part_q, sib_q, sum_q, code_q, ctop_q, rec_q, rtop_q,
    part_k, sib_k, sum_k, code_k, ctop_k, rec_k, rtop_k,
    part_t, sib_t, sum_t, code_t, ctop_t, rec_t, rtop_t,
    sems, lsem,
):
    y, z, c, x = (lax.axis_index(name) for name in ("y", "z", "c", "head"))
    used = [0]

    def at_y(dy, other=False):
        return (lax.rem(y + dy, NY), z, 1 - c if other else c, x)

    def at_z(dz):
        return (y, lax.rem(z + dz, NZ), c, x)

    def at_x(dx):
        return (y, z, c, lax.rem(x + dx, NX))

    sibling = (y, z, 1 - c, x)
    y_order = (1, 3, 2)
    z_order = (4, 3, 5, 2, 6, 1, 7)

    def send(src, dst, device):
        i = used[0]
        used[0] += 2
        copy = pltpu.make_async_remote_copy(
            src_ref=src, dst_ref=dst, send_sem=sems.at[i], recv_sem=sems.at[i + 1],
            device_id=device, device_id_type=MESH,
        )
        copy.start()
        started.append(copy)
        return copy

    started = []

    def arrived(copies):
        for copy in copies:
            copy.wait_recv()

    loads = []
    for i, (src, dst) in enumerate(
        (
            (g_hbm.at[y, :, c], gs),
            (u_hbm.at[y, :, c], us),
            (w_hbm.at[:, pl.ds(pl.multiple_of(y * 128, 128), 128)], wcol),
        )
    ):
        copy = pltpu.make_async_copy(src, dst, lsem.at[i])
        copy.start()
        loads.append(copy)

    barrier = pltpu.get_barrier_semaphore()
    partners = [sibling]
    partners += [at_y(d) for d in (1, 2, 3)] + [at_y(d, True) for d in (1, 2, 3)]
    partners += [at_z(d) for d in range(1, NZ)] + [at_x(d) for d in (1, 2, 3)]
    for device in partners:
        pl.semaphore_signal(barrier, inc=1, device_id=device, device_id_type=MESH)
    me = 2 * y + c
    first = c == 0
    rate_full = as_columns(rate_ref[...], 4)
    target = -(rate_full * v_ref[...])
    own_tops = []
    for buffer, codes, value in ((k2, kc, k_ref[...]), (t2, tc, target), (q2, qc, q_ref[...])):
        top = row_top(value)
        codes[me] = encode(value, top)
        own_tops.append(as_row(top * (1.0 / SPAN)))
        hi, lo = halves(value)
        buffer[me, 0] = hi
        buffer[me, 1] = lo
    tops_s[...] = jnp.concatenate(own_tops + [jnp.zeros((5, TOK), F32)], axis=0)
    tops[me] = jnp.ones((8, TOK), F32)
    tokens = pl.ds(pl.multiple_of(c * TOK, TOK), TOK)
    grads[x, tokens, :] = ograd_ref[...]

    pl.semaphore_wait(barrier, len(partners))

    osib = send(
        oproj_ref.at[:, pl.ds(pl.multiple_of((1 - c) * 256, 256), 256)], oproj_sib, sibling
    )
    xs = [send(grads.at[x, tokens], grads.at[x, tokens], at_x(d)) for d in (1, 3, 2)]
    gsib = [send(grads.at[x, tokens], grads.at[x, tokens], sibling)]
    tsends = [send(tops_s, tops.at[me], sibling)]
    tsends += [send(tops_s, tops.at[me], at_y(d)) for d in (1, 2, 3)]
    tsends += [send(tops_s, tops.at[me], at_y(d, True)) for d in (1, 2, 3)]

    def to_y(codes):
        return [send(codes.at[me], codes.at[me], at_y(d)) for d in y_order]

    def forward(codes, copies):
        result = []
        for d, copy in zip(y_order, copies):
            copy.wait_recv()
            block = 2 * lax.rem(y + NY - d, NY) + c
            result.append(send(codes.at[block], codes.at[block], sibling))
        return result

    def open_blocks(buffer, codes, core):
        for d in (1, 2, 3, 0) if core is not c else (1, 2, 3):
            block = 2 * lax.rem(y + d, NY) + core
            hi, lo = halves(decode(codes[block]))
            buffer[block, 0] = hi
            buffer[block, 1] = lo

    osib.wait_recv()
    own = oproj_ref[:, pl.ds(pl.multiple_of(c * 256, 256), 256)]
    yrows = pl.multiple_of(y * 128, 128)
    oall[z, pl.ds(pl.multiple_of(yrows + c * 64, 64), 64)] = own
    oall[z, pl.ds(pl.multiple_of(yrows + (1 - c) * 64, 64), 64)] = oproj_sib[...]
    ohere = oall.at[z, pl.ds(yrows, 128)]
    oy = [send(ohere, ohere, at_y(d)) for d in y_order]
    ky = to_y(kc)
    ty = to_y(tc)
    ksib = [send(kc.at[me], kc.at[me], sibling)]
    tsib = [send(tc.at[me], tc.at[me], sibling)]

    for copy in loads:
        copy.wait()
    wt = wcol[...].T.reshape(NZ, 2, 8, D)
    wts[...] = jnp.where(first, wt[:, 0], wt[:, 1])

    def ring(step, previous):
        result = {}
        for half in (0, 1):
            for way in (1, -1):
                if step == 4 and (half == 0) != (way == 1):
                    continue
                if previous is not None:
                    previous[half, way].wait_recv()
                block = lax.rem(z + NZ - way * (step - 1), NZ)
                part = oall.at[block, pl.ds(256 * half, 256)]
                result[half, way] = send(part, part, at_z((way + NZ) % NZ))
        if step == 4:
            for key in ((1, 1), (0, -1)):
                previous[key].wait_recv()
        return result

    arrived(oy)
    r1st = ring(1, None)
    r2nd = ring(2, r1st)
    ksib += forward(kc, ky)
    tsib += forward(tc, ty)
    qy = to_y(qc)
    qsib = [send(qc.at[me], qc.at[me], sibling)]
    open_blocks(k2, kc, c)
    open_blocks(t2, tc, c)
    r3rd = ring(3, r2nd)
    arrived(ksib)
    open_blocks(k2, kc, 1 - c)
    arrived(tsib)
    open_blocks(t2, tc, 1 - c)
    arrived(tsends)

    def scale_row(i):
        return jnp.concatenate([tops[b, i : i + 1] for b in range(8)], axis=1)

    k_scale, t_scale = scale_row(0), scale_row(1)

    def flat(ref):
        return ref[...].reshape(FS, D)

    def whole(buffer):
        return tuple(buffer[:, i].reshape(8 * TOK, D) for i in (0, 1))

    def silu_parts(before):
        sigma = jax.nn.sigmoid(before)
        return sigma, before * sigma, sigma * (1.0 + before * (1.0 - sigma))

    with jax.named_scope("partials"):
        both = k_scale * three(
            dot_nt, jnp.concatenate([flat(gs), flat(us)], axis=0), *whole(k2)
        )
        before, linear = both[:FS], both[FS:]
        hgrad = t_scale * three(dot_nt, flat(wts), *whole(t2))
        before_s[...] = before
        linear_s[...] = linear
        hgrad_s[...] = hgrad
        sigma, act, dsilu = silu_parts(before)
        pgu = three(
            dot_nn,
            k_scale * jnp.concatenate([hgrad * linear * dsilu, hgrad * act], axis=0),
            *whole(k2),
        )
        pd = three(dot_nn, t_scale * (act * linear), *whole(t2))

    def fill(plain, codes, gu, down):
        parts = [v.reshape(NZ, 8, D) for v in (gu[:FS], gu[FS:], down)]
        for i in range(3):
            plain[i] = parts[i]
        wide, thin, scales = pack(*parts)
        codes[:, :, 0:512] = wide
        codes[:, :, 512:768] = thin
        codes[:, :, 768:896] = scales

    def scatter_z(src, dst):
        return [
            send(src.at[lax.rem(z + d, NZ)], dst.at[z], at_z(d)) for d in z_order
        ]

    def summed(plain, dst, copies):
        value = [plain[i, z] for i in range(3)]
        for d, copy in zip(z_order, copies):
            copy.wait_recv()
            more = unpack(dst[pl.ds(lax.rem(z + NZ - d, NZ), 1)])
            value = [a + b[0] for a, b in zip(value, more)]
        return value

    def gather_z(codes, value):
        wide, thin, scales = pack(*(v[None] for v in value))
        codes[z, :, 0:512] = wide[0]
        codes[z, :, 512:768] = thin[0]
        codes[z, :, 768:896] = scales[0]
        return [send(codes.at[z], codes.at[z], at_z(d)) for d in z_order]

    def fold(row):
        return row[:, 0:128] + row[:, 128:256] + row[:, 256:384] + row[:, 384:512]

    def cut(row):
        return [row[:, 128 * i : 128 * (i + 1)] for i in range(4)]

    def uncut(stats, at):
        return jnp.concatenate([stats[at + i : at + i + 1] for i in range(4)], axis=1)

    def plane_start(st, sty, rows):
        value = jnp.concatenate(rows + [jnp.zeros((16 - len(rows), 128), F32)], axis=0)
        st[...] = value
        sty[me] = value
        sends = [send(st, sty.at[me], at_y(d)) for d in (2, 1, 3)]
        sends += [send(st, sty.at[me], at_y(d, True)) for d in (2, 1, 3)]
        return sends + [send(st, sty.at[me], sibling)]

    def plane_finish(sends, sty, sts, stz):
        arrived(sends)
        group = jnp.sum(sty[...], axis=0)
        sts[...] = group
        stz[z] = group
        return [send(sts, stz.at[z], at_z(d)) for d in z_order]

    fill(s1, c1, pgu, pd)
    rs1 = scatter_z(c1, r1)

    for d, copy in zip((1, 3, 2), xs):
        copy.wait_recv()
        src = lax.rem(x + NX - d, NX)
        gsib.append(send(grads.at[src, tokens], grads.at[src, tokens], sibling))
    r4th = ring(4, r3rd)
    qsib += forward(qc, qy)
    open_blocks(q2, qc, c)

    pg_c, pu_c, pd_c = summed(s1, r1, rs1)
    ag1 = gather_z(a1, (pg_c, pu_c, pd_c))
    gc, uc, wc = gs[z], us[z], wts[z]
    ys1 = plane_start(
        st1, sty1,
        [fold(col_sum(pg_c * pg_c)), fold(col_sum(pu_c * pu_c))]
        + cut(col_sum(pd_c * pd_c)) + cut(col_sum(wc * pd_c)) + cut(col_sum(wc * wc)),
    )

    arrived(gsib)
    arrived(r4th.values())
    cot = jnp.zeros((256, 256), F32)
    for i in range(NZ):
        both = jnp.concatenate(
            [grads[j, :, 128 * i : 128 * (i + 1)] for j in range(NX)], axis=1
        )
        cot = cot + dot_nn(both, oall[i])
    rows = pl.ds(2 * y, 2)

    def half(core):
        return pl.ds(pl.multiple_of(core * 256, 256), 256)

    cot_top = row_top(cot)
    oc[rows, :, half(c)] = encode(cot, cot_top).reshape(2, TOK, 256)
    for j in (0, 1):
        otops[c, 2 * y + j] = jnp.broadcast_to(
            as_row(cot_top[TOK * j : TOK * (j + 1)] * (1.0 / SPAN)), (8, TOK)
        )
    tops_here = otops.at[c, rows]
    here = oc.at[rows, :, half(c)]
    otsends = [send(tops_here, tops_here, at_y(d)) for d in y_order]
    otsends += [send(tops_here, tops_here, at_y(d, True)) for d in y_order]
    otsends += [send(tops_here, tops_here, sibling)]
    coty = [send(here, here, at_y(d)) for d in y_order]
    cotsib = [send(here, here, sibling)]
    cot_hi, cot_lo = halves(cot)
    o2[rows, 0, :, half(c)] = cot_hi.reshape(2, TOK, 256)
    o2[rows, 1, :, half(c)] = cot_lo.reshape(2, TOK, 256)

    zs1 = plane_finish(ys1, sty1, sts1, stz1)

    arrived(qsib)
    open_blocks(q2, qc, 1 - c)
    q_scale = scale_row(2)
    for d, copy in zip(y_order, coty):
        copy.wait_recv()
        there = oc.at[pl.ds(2 * lax.rem(y + NY - d, NY), 2), :, half(c)]
        cotsib.append(send(there, there, sibling))

    def open_cot(core):
        for d in (1, 2, 3, 0) if core is not c else (1, 2, 3):
            for j in (0, 1):
                block = 2 * lax.rem(y + d, NY) + j
                scale = as_columns(otops[core, block][0:1], 2)
                hi, lo = halves(decode(oc[block, :, half(core)]) * scale)
                o2[block, 0, :, half(core)] = hi
                o2[block, 1, :, half(core)] = lo

    arrived(otsends)
    open_cot(c)
    arrived(cotsib)
    open_cot(1 - c)
    arrived(zs1)
    arrived(ag1)

    with jax.named_scope("renormed"):
        stats = jnp.sum(stz1[...], axis=0)
        d_pp, d_wp, d_ww = uncut(stats, 2), uncut(stats, 6), uncut(stats, 10)
        pn_g = jnp.sqrt(total(stats[0:1]) + EPS)
        pn_u = jnp.sqrt(total(stats[1:2]) + EPS)
        pn_d = jnp.sqrt(total(d_pp) + EPS)
        k_g, k_u, k_d = SCALE / pn_g, SCALE / pn_u, SCALE / pn_d
        old_d = jnp.sqrt(d_ww + EPS)
        new_d = jnp.sqrt(
            jnp.maximum(d_ww - 2.0 * k_d * d_wp + k_d * k_d * d_pp, 0.0) + EPS
        )
        d_pm = d_wp - k_d * d_pp

        def moved_rows(matrix, partial, k):
            moved = matrix - partial * k
            old = jnp.sqrt(row_sum(matrix * matrix) + EPS)
            new = jnp.sqrt(row_sum(moved * moved) + EPS)
            return moved, old, new

        g_m, u_m, w_m = flat(gs), flat(us), flat(wts)
        p_g, p_u, p_d = (v.reshape(FS, D) for v in unpack(a1[...]))
        mv_g, old_g, new_g = moved_rows(g_m, p_g, k_g)
        mv_u, old_u, new_u = moved_rows(u_m, p_u, k_u)
        mv_d = w_m - p_d * k_d
        ren_gu = jnp.concatenate([mv_g * (old_g / new_g), mv_u * (old_u / new_u)], axis=0)
        ren_d = mv_d * (old_d / new_d)

    with jax.named_scope("cotangents"):
        both = q_scale * three(dot_nt, ren_gu, *whole(q2))
        before, linear = both[:FS], both[FS:]
        hcot = three(dot_nt, ren_d, *whole(o2))
        sigma, act, dsilu = silu_parts(before)
        acts_q = jnp.concatenate([hcot * linear * dsilu, hcot * act], axis=0)
        cgu = three(dot_nn, q_scale * acts_q, *whole(q2))
        cd = three(dot_nn, act * linear, *whole(o2))
        fill(s2, c2, cgu, cd)
    rs2 = scatter_z(c2, r2)
    with jax.named_scope("query_grad"):
        part_q[...] = back(acts_q, ren_gu).reshape(NY, 2, TOK, D)
    sibq = send(part_q.at[:, 1 - c], sib_q, sibling)

    cg_c, cu_c, cd_c = summed(s2, r2, rs2)
    ag2 = gather_z(a2, (cg_c, cu_c, cd_c))

    def row_back(matrix, partial, k, grad):
        moved, old, new = moved_rows(matrix, partial, k)
        along = row_sum(moved * grad)
        moved_grad = (old / new) * (grad - moved * (along / (new * new)))
        return moved_grad, moved_grad + (along / (new * old)) * matrix

    mg_c, direct_g = row_back(gc, pg_c, k_g, cg_c)
    mu_c, direct_u = row_back(uc, pu_c, k_u, cu_c)
    ys2 = plane_start(
        st2, sty2,
        [fold(-col_sum(pg_c * mg_c)), fold(-col_sum(pu_c * mu_c))]
        + cut(col_sum((wc - pd_c * k_d) * cd_c)) + cut(col_sum(pd_c * cd_c)),
    )

    def to_owner(part, sib, plain, codes, scales, rec, rec_scales, copy):
        copy.wait_recv()
        value = part[:, c] + sib[...]
        plain[...] = value
        top = row_top(value)
        codes[...] = encode(value, top)
        for i in range(NY):
            scales[i] = jnp.broadcast_to(as_row(top[i] * (1.0 / SPAN)), (8, TOK))
        sends = []
        for d in y_order:
            to = lax.rem(y + d, NY)
            sends.append(
                (
                    send(codes.at[to], rec.at[y], at_y(d)),
                    send(scales.at[to], rec_scales.at[y], at_y(d)),
                )
            )
        return sends

    def owned(plain, rec, rec_scales, copies):
        value = plain[y]
        for d, pair in zip(y_order, copies):
            arrived(pair)
            src = lax.rem(y + NY - d, NY)
            value = value + decode(rec[src]) * as_columns(rec_scales[src][0:1], 4)
        return value

    yq = to_owner(part_q, sib_q, sum_q, code_q, ctop_q, rec_q, rtop_q, sibq)
    zs2 = plane_finish(ys2, sty2, sts2, stz2)

    arrived(zs2)
    arrived(ag2)
    with jax.named_scope("direction"):
        stats2 = jnp.sum(stz2[...], axis=0)
        inner_g, inner_u = total(stats2[0:1]), total(stats2[1:2])
        along_d, d_pg = uncut(stats2, 2), uncut(stats2, 6)
        ratio_d = old_d / new_d
        shrink_d = along_d / (new_d * new_d)
        inner_d = -total(ratio_d * (d_pg - d_pm * shrink_d))
        c_g, c_u, c_d = (v.reshape(FS, D) for v in unpack(a2[...]))
        mgrad_g, _ = row_back(g_m, p_g, k_g, c_g)
        mgrad_u, _ = row_back(u_m, p_u, k_u, c_u)
        mgrad_d = ratio_d * (c_d - mv_d * shrink_d)
        direct_d = mgrad_d + (along_d / (new_d * old_d)) * w_m
        dir_g = -k_g * (mgrad_g + p_g * (inner_g / (pn_g * pn_g)))
        dir_u = -k_u * (mgrad_u + p_u * (inner_u / (pn_u * pn_u)))
        dir_d = -k_d * (mgrad_d + p_d * (inner_d / (pn_d * pn_d)))

    with jax.named_scope("through"):
        both = k_scale * three(dot_nt, jnp.concatenate([dir_g, dir_u], axis=0), *whole(k2))
        d_bg, d_lg = both[:FS], both[FS:]
        d_hid = t_scale * three(dot_nt, dir_d, *whole(t2))
        before, linear, hgrad = before_s[...], linear_s[...], hgrad_s[...]
        sigma, act, dsilu = silu_parts(before)
        curve = sigma * (1.0 - sigma) * (2.0 + before * (1.0 - 2.0 * sigma))
        d_h = d_bg * linear * dsilu + d_lg * act
        d_l = d_bg * hgrad * dsilu + d_hid * act
        d_b = d_bg * hgrad * linear * curve + (d_lg * hgrad + d_hid * linear) * dsilu
        part_t[...] = back(
            jnp.concatenate([act * linear, d_h], axis=0),
            jnp.concatenate([dir_d, w_m], axis=0),
        ).reshape(NY, 2, TOK, D)
        sibt = send(part_t.at[:, 1 - c], sib_t, sibling)
        part_k[...] = back(
            jnp.concatenate([hgrad * linear * dsilu, hgrad * act, d_b, d_l], axis=0),
            jnp.concatenate([dir_g, dir_u, g_m, u_m], axis=0),
        ).reshape(NY, 2, TOK, D)
        sibk = send(part_k.at[:, 1 - c], sib_k, sibling)
        yt = to_owner(part_t, sib_t, sum_t, code_t, ctop_t, rec_t, rtop_t, sibt)
        th_d = three(dot_nn, t_scale * d_h, *whole(t2))
        th_d = th_d + jnp.where(z == 0, direct_d, jnp.zeros_like(direct_d))
        th_d = th_d.reshape(NZ, 1, 8, D)
        none = jnp.zeros_like(th_d)
        th_d = jnp.concatenate(
            [jnp.where(first, th_d, none), jnp.where(first, none, th_d)], axis=1
        ).reshape(2 * FS, D)
        th_t = th_d.T.reshape(NY, NZ, 2, 8, 2 * FS)
        for i in range(NZ):
            d3[i] = th_t[:, i].reshape(8, 8, 2 * FS)
        rsd = scatter_z(d3, rd3)
        yk = to_owner(part_k, sib_k, sum_k, code_k, ctop_k, rec_k, rtop_k, sibk)
        th_gu = three(dot_nn, k_scale * jnp.concatenate([d_b, d_l], axis=0), *whole(k2))
        th_gu = jnp.concatenate(
            [th_gu[:FS].reshape(NZ, 8, D), th_gu[FS:].reshape(NZ, 8, D)], axis=1
        )
        s3[...] = th_gu
        top_bf = (row_top(th_gu) * 1.01).astype(BF16)
        top = top_bf.astype(F32)
        c3[:, :, 0:512] = encode(th_gu, top)
        c3[:, :, 512:640] = jnp.broadcast_to(top, (NZ, 16, 128)).astype(BF16)
        rs3 = scatter_z(c3, r3)

    qg_ref[...] = owned(sum_q, rec_q, rtop_q, yq)
    down = d3[z]
    for d, copy in zip(z_order, rsd):
        copy.wait_recv()
        down = down + rd3[lax.rem(z + NZ - d, NZ)]
    ds3[...] = down
    dr3[me] = ds3[me]
    fin = [send(ds3.at[2 * y + 1 - c], dr3.at[me], sibling)]
    for d in (1, 2, 3):
        to = 2 * lax.rem(y + d, NY)
        fin.append(send(ds3.at[to + c], dr3.at[me], at_y(d)))
        fin.append(send(ds3.at[to + 1 - c], dr3.at[me], at_y(d, True)))
    vg_ref[...] = -(rate_full * owned(sum_t, rec_t, rtop_t, yt))
    kg_ref[...] = owned(sum_k, rec_k, rtop_k, yk)
    gate_up = s3[z]
    for d, copy in zip(z_order, rs3):
        copy.wait_recv()
        codes = r3[lax.rem(z + NZ - d, NZ)]
        gate_up = gate_up + decode(codes[:, 0:512]) * (
            codes[:, 512:640].astype(F32)[:, 0:1] * (1.0 / SPAN)
        )
    gg_ref[...] = gate_up[0:8] + direct_g
    ug_ref[...] = gate_up[8:16] + direct_u
    arrived(fin)
    dg_ref[...] = jnp.concatenate(
        [dr3[2 * i] + dr3[2 * i + 1] for i in range(NY)], axis=1
    )
    for copy in started:
        copy.wait_send()


def hand_over(*refs):
    sems = refs[-1]
    copies = [pltpu.make_async_copy(refs[i], refs[6 + i], sems.at[i]) for i in range(6)]
    for copy in copies:
        copy.start()
    for copy in copies:
        copy.wait()


def body(queries, keys, values, rates, gate_fast, up_fast, down_fast, out_proj, out_grad):
    vmem = pl.BlockSpec(memory_space=pltpu.VMEM)
    hbm = pl.BlockSpec(memory_space=pl.ANY)

    def buf(*shape, dtype=F32):
        return pltpu.VMEM(shape, dtype)

    exchange = [
        buf(3, NZ, 8, D), *[buf(NZ, 16, 896, dtype=BF16)] * 3,
        buf(16, 128), buf(8, 16, 128), buf(16, 128), buf(NZ, 16, 128),
    ]
    grads = [
        buf(NY, 2, TOK, D), buf(NY, TOK, D), buf(NY, TOK, D),
        buf(NY, TOK, D, dtype=BF16), buf(NY, 8, TOK),
        buf(NY, TOK, D, dtype=BF16), buf(NY, 8, TOK),
    ]
    outs = pl.pallas_call(
        kernel,
        out_shape=[jax.ShapeDtypeStruct((TOK, D), F32)] * 3
        + [jax.ShapeDtypeStruct((8, D), F32)] * 3,
        in_specs=[vmem] * 4 + [hbm] * 3 + [vmem] * 2,
        out_specs=[vmem] * 6,
        scratch_shapes=[buf(8, 2, TOK, D, dtype=BF16)] * 4
        + [buf(8, TOK, D, dtype=BF16)] * 4
        + [
            buf(8, TOK), buf(8, 8, TOK), buf(2, 8, 8, TOK),
            buf(64, 256, dtype=BF16),
            buf(NZ, 512, 256, dtype=BF16),
            buf(NX, 256, 1024, dtype=BF16),
            buf(NZ, 8, D), buf(NZ, 8, D), buf(D, 128), buf(NZ, 8, D),
        ]
        + [buf(FS, 8 * TOK)] * 3
        + exchange
        + exchange
        + [
            buf(NZ, 16, D), *[buf(NZ, 16, 640, dtype=BF16)] * 2,
            buf(NZ, 8, 8, 128), buf(NZ, 8, 8, 128), buf(8, 8, 128), buf(8, 8, 128),
        ]
        + grads * 3
        + [pltpu.SemaphoreType.DMA((420,)), pltpu.SemaphoreType.DMA((3,))],
        compiler_params=pltpu.CompilerParams(
            collective_id=0, has_side_effects=True, vmem_limit_bytes=58 * 2**20
        ),
    )(
        queries, keys, values, rates,
        gate_fast.reshape(NY, NZ, 2, 8, D), up_fast.reshape(NY, NZ, 2, 8, D),
        down_fast.reshape(D, D), out_proj.T, out_grad,
    )
    outs = pl.pallas_call(
        hand_over,
        out_shape=[jax.ShapeDtypeStruct(o.shape, F32) for o in outs],
        in_specs=[hbm] * 6,
        out_specs=[hbm] * 6,
        scratch_shapes=[pltpu.SemaphoreType.DMA((6,))],
    )(*outs)
    return (*outs[:3], *(o.reshape(1, 8, D) for o in outs[3:]))


def solution(mesh):
    torus = Mesh(mesh.devices.reshape(NY, NZ, NC, NX), ("y", "z", "c", "head"))
    return jax.shard_map(
        body,
        mesh=torus,
        in_specs=(
            P(SEQ, "head"), P(SEQ, "head"), P(SEQ, "head"), P("head", SEQ),
            P("head", None, None), P("head", None, None), P("head", None, None),
            P("head", SEQ), P(SEQ, "head"),
        ),
        out_specs=(
            P(SEQ, "head"), P(SEQ, "head"), P(SEQ, "head"),
            P("head", SEQ, None), P("head", SEQ, None), P("head", SEQ, None),
        ),
        check_vma=False,
    )
```

```python
import math

import jax
import jax.numpy as jnp
from jax import lax
from jax.experimental import pallas as pl
from jax.experimental.pallas import tpu as pltpu
from jax.sharding import Mesh
from jax.sharding import PartitionSpec as P

MESH = pl.DeviceIdType.MESH
SEQ = ("y", "z", "c")
F32 = jnp.float32
BF16 = jnp.bfloat16
NY, NZ, NC, NX = 4, 8, 2, 4
TOK = 128
D = 512
FS = 64
SCALE = 0.3 * math.sqrt(512)
EPS = 1e-06
SPAN = 251.0
LOW = 125.0
LN2 = math.log(2.0)
STEP = 1.0 / (SPAN * LN2)


def halves(x):
    hi = x.astype(BF16)
    return hi, (x - hi.astype(F32)).astype(BF16)


def dot_nt(a, b):
    return lax.dot_general(a, b, (((1,), (1,)), ((), ())), preferred_element_type=F32)


def dot_nn(a, b):
    return lax.dot_general(a, b, (((1,), (0,)), ((), ())), preferred_element_type=F32)


def dot_tn(a, b):
    return lax.dot_general(a, b, (((0,), (0,)), ((), ())), preferred_element_type=F32)


def three(product, a, b_hi, b_lo):
    hi, lo = halves(a)
    n = a.shape[0]
    both = product(jnp.concatenate([hi, lo], axis=0), b_hi)
    return both[:n] + both[n:] + product(hi, b_lo)


def back(acts, mats):
    a_hi, a_lo = halves(acts)
    m_hi, m_lo = halves(mats)
    return dot_tn(
        jnp.concatenate([a_hi, a_lo, a_hi], axis=0), jnp.concatenate([m_hi, m_hi, m_lo], axis=0)
    )


def encode(x, top):
    size = jnp.exp(jnp.abs(x) * (SPAN * LN2 / top) - LOW * LN2)
    return jnp.where(x < 0, -size, size).astype(BF16)


def decode(codes):
    value = codes.astype(F32)
    size = jnp.log(jnp.abs(value)) + LOW * LN2
    return jnp.where(value < 0, -size, size)


def row_top(x):
    return jnp.maximum(jnp.max(jnp.abs(x), axis=-1, keepdims=True), 1e-30)


def as_row(column):
    return jnp.broadcast_to(column, (TOK, TOK)).T[0:1]


def as_columns(row, tiles):
    return jnp.concatenate([jnp.broadcast_to(row, (TOK, TOK)).T] * tiles, axis=1)


def pack(gate, up, down):
    wide = jnp.concatenate([gate, up], axis=1)
    thin = jnp.concatenate([down[..., :256], down[..., 256:]], axis=1)
    top_w = (row_top(wide) * 1.01).astype(BF16)
    top_t = (row_top(thin) * 1.01).astype(BF16)
    top_w32, top_t32 = top_w.astype(F32), top_t.astype(F32)
    lanes = (*wide.shape[:2], 64)
    tops = jnp.concatenate(
        [jnp.broadcast_to(top_w32, lanes), jnp.broadcast_to(top_t32, lanes)], axis=2
    ).astype(BF16)
    return encode(wide, top_w32), encode(thin, top_t32), tops


def unpack(codes):
    tops = codes[..., 768:896].astype(F32) * STEP
    wide = decode(codes[..., :512]) * tops[..., 0:1]
    thin = decode(codes[..., 512:768]) * tops[..., 64:65]
    down = jnp.concatenate([thin[:, :8], thin[:, 8:]], axis=2)
    return wide[:, :8], wide[:, 8:], down


def row_sum(x):
    return jnp.sum(x, axis=1, keepdims=True)


def col_sum(x):
    return jnp.sum(x, axis=0, keepdims=True)


def total(x):
    return jnp.sum(jnp.sum(x, axis=1, keepdims=True), axis=0, keepdims=True)


def kernel(
    q_ref, k_ref, v_ref, rate_ref, g_hbm, u_hbm, w_hbm, oproj_ref, ograd_ref,
    qg_ref, kg_ref, vg_ref, gg_ref, ug_ref, dg_ref,
    k1, t1, k2, t2, q2, o2, kc, tc, qc, oc, tops_s, tops, otops, oproj_sib, oall, grads,
    gs, us, wcol, wts,
    before_s, linear_s, hgrad_s,
    p1, pc1, pr1, s1, c1, r1, a1, st1, sty1, sts1, stz1,
    s2, c2, r2, a2, st2, sty2, sts2, stz2,
    s3, c3, r3, d3, rd3, ds3, dr3,
    part_q, sib_q, sum_q, code_q, ctop_q, rec_q, rtop_q,
    part_k, sib_k, sum_k, code_k, ctop_k, rec_k, rtop_k,
    part_t, sib_t, sum_t, code_t, ctop_t, rec_t, rtop_t,
    sems, lsem,
):
    y, z, c, x = (lax.axis_index(name) for name in ("y", "z", "c", "head"))
    used = [0]

    def at_y(dy, other=False):
        return (lax.rem(y + dy, NY), z, 1 - c if other else c, x)

    def at_z(dz):
        return (y, lax.rem(z + dz, NZ), c, x)

    def at_x(dx):
        return (y, z, c, lax.rem(x + dx, NX))

    sibling = (y, z, 1 - c, x)
    y_order = (1, 3, 2)
    z_order = (4, 3, 5, 2, 6, 1, 7)

    def send(src, dst, device):
        i = used[0]
        used[0] += 2
        copy = pltpu.make_async_remote_copy(
            src_ref=src, dst_ref=dst, send_sem=sems.at[i], recv_sem=sems.at[i + 1],
            device_id=device, device_id_type=MESH,
        )
        copy.start()
        started.append(copy)
        return copy

    started = []

    def arrived(copies):
        for copy in copies:
            copy.wait_recv()

    loads = []
    for i, (src, dst) in enumerate(
        (
            (g_hbm.at[:, :, c], gs),
            (u_hbm.at[:, :, c], us),
            (w_hbm, wcol),
        )
    ):
        copy = pltpu.make_async_copy(src, dst, lsem.at[i])
        copy.start()
        loads.append(copy)

    barrier = pltpu.get_barrier_semaphore()
    partners = [sibling]
    partners += [at_y(d) for d in (1, 2, 3)] + [at_y(d, True) for d in (1, 2, 3)]
    partners += [at_z(d) for d in range(1, NZ)] + [at_x(d) for d in (1, 2, 3)]
    for device in partners:
        pl.semaphore_signal(barrier, inc=1, device_id=device, device_id_type=MESH)
    me = 2 * y + c
    first = c == 0
    rate_full = as_columns(rate_ref[...], 4)
    target = -(rate_full * v_ref[...])
    for near, value in ((k1, k_ref[...]), (t1, target)):
        for i, part in enumerate(halves(value)):
            near[c, i] = part
    tokens = pl.ds(pl.multiple_of(c * TOK, TOK), TOK)
    grads[x, tokens, :] = ograd_ref[...]
    for copy in loads:
        copy.wait()
    wt = wcol[...].T.reshape(NY, NZ, 2, 8, D)
    wts[...] = jnp.where(first, wt[:, :, 0], wt[:, :, 1])

    pl.semaphore_wait(barrier, len(partners))

    osib = send(
        oproj_ref.at[:, pl.ds(pl.multiple_of((1 - c) * 256, 256), 256)], oproj_sib, sibling
    )
    near = [send(k1.at[c], k1.at[c], sibling), send(t1.at[c], t1.at[c], sibling)]
    xs = [send(grads.at[x, tokens], grads.at[x, tokens], at_x(d)) for d in (1, 3, 2)]
    gsib = [send(grads.at[x, tokens], grads.at[x, tokens], sibling)]
    def to_y(codes):
        return {d: send(codes.at[me], codes.at[me], at_y(d)) for d in y_order}

    def open_blocks(buffer, codes, copies):
        result = []
        for d in y_order:
            copies[d].wait_recv()
            block = 2 * lax.rem(y + NY - d, NY) + c
            for i, part in enumerate(halves(decode(codes[block]))):
                buffer[block, i] = part
            result.append(send(buffer.at[block], buffer.at[block], sibling))
        return result

    osib.wait_recv()
    own = oproj_ref[:, pl.ds(pl.multiple_of(c * 256, 256), 256)]
    yrows = pl.multiple_of(y * 128, 128)
    oall[z, pl.ds(pl.multiple_of(yrows + c * 64, 64), 64)] = own
    oall[z, pl.ds(pl.multiple_of(yrows + (1 - c) * 64, 64), 64)] = oproj_sib[...]
    ohere = oall.at[z, pl.ds(yrows, 128)]
    oy = [send(ohere, ohere, at_y(d)) for d in y_order]
    def ring(step, previous):
        result = {}
        for half in (0, 1):
            for way in (1, -1):
                if step == 4 and (half == 0) != (way == 1):
                    continue
                if previous is not None:
                    previous[half, way].wait_recv()
                block = lax.rem(z + NZ - way * (step - 1), NZ)
                part = oall.at[block, pl.ds(256 * half, 256)]
                result[half, way] = send(part, part, at_z((way + NZ) % NZ))
        if step == 4:
            for key in ((1, 1), (0, -1)):
                previous[key].wait_recv()
        return result

    def scale_row(i):
        return jnp.concatenate([tops[b, i : i + 1] for b in range(8)], axis=1)

    def flat(ref):
        return ref[y].reshape(FS, D)

    def whole(buffer):
        return tuple(buffer[:, i].reshape(8 * TOK, D) for i in (0, 1))

    def silu_parts(before):
        sigma = jax.nn.sigmoid(before)
        return sigma, before * sigma, sigma * (1.0 + before * (1.0 - sigma))

    arrived(near)
    with jax.named_scope("partials"):
        k_near = tuple(k1[:, i].reshape(2 * TOK, D) for i in (0, 1))
        t_near = tuple(t1[:, i].reshape(2 * TOK, D) for i in (0, 1))
        n = NY * FS
        both = three(
            dot_nt,
            jnp.concatenate([gs[...].reshape(n, D), us[...].reshape(n, D)], axis=0),
            *k_near,
        )
        before, linear = both[:n], both[n:]
        hgrad = three(dot_nt, wts[...].reshape(n, D), *t_near)
    arrived(oy)
    r1st = ring(1, None)
    with jax.named_scope("partials"):
        sigma, act, dsilu = silu_parts(before)
        pgu = three(
            dot_nn, jnp.concatenate([hgrad * linear * dsilu, hgrad * act], axis=0), *k_near
        )
        p1[0] = pgu[:n].reshape(NY, NZ, 8, D)
        p1[1] = pgu[n:].reshape(NY, NZ, 8, D)
        p1[2] = three(dot_nn, act * linear, *t_near).reshape(NY, NZ, 8, D)

    def put(codes, index, values):
        wide, thin, scales = pack(*values)
        codes[index, :, :, 0:512] = wide
        codes[index, :, :, 512:768] = thin
        codes[index, :, :, 768:896] = scales

    py = {}
    for d in (2, 1, 3):
        to = lax.rem(y + d, NY)
        put(pc1, to, tuple(p1[i, to] for i in range(3)))
        py[d] = send(pc1.at[to], pr1.at[y], at_y(d))
    r2nd = ring(2, r1st)

    own_tops = []
    for buffer, near, codes, value in (
        (k2, k1, kc, k_ref[...]), (t2, t1, tc, target), (q2, None, qc, q_ref[...])
    ):
        top = row_top(value)
        codes[me] = encode(value, top)
        own_tops.append(as_row(top * STEP))
        if near is None:
            for i, part in enumerate(halves(value)):
                buffer[me, i] = part
        else:
            buffer[pl.ds(2 * y, 2)] = near[...]
    tops_s[...] = jnp.concatenate(own_tops + [jnp.zeros((5, TOK), F32)], axis=0)
    tops[pl.ds(2 * y, 2)] = jnp.ones((2, 8, TOK), F32)
    tsends = [send(tops_s, tops.at[me], at_y(d)) for d in (1, 2, 3)]
    tsends += [send(tops_s, tops.at[me], at_y(d, True)) for d in (1, 2, 3)]
    qsib = [send(q2.at[me], q2.at[me], sibling)]

    def fill(plain, codes, parts):
        for i in range(3):
            plain[i] = parts[i]
        wide, thin, scales = pack(*parts)
        codes[:, :, 0:512] = wide
        codes[:, :, 512:768] = thin
        codes[:, :, 768:896] = scales

    def scatter_z(src, dst):
        return [
            send(src.at[lax.rem(z + d, NZ)], dst.at[z], at_z(d)) for d in z_order
        ]

    def summed(plain, dst, copies):
        value = [plain[i, z] for i in range(3)]
        for d, copy in zip(z_order, copies):
            copy.wait_recv()
            more = unpack(dst[pl.ds(lax.rem(z + NZ - d, NZ), 1)])
            value = [a + b[0] for a, b in zip(value, more)]
        return value

    def gather_z(codes, value):
        wide, thin, scales = pack(*(v[None] for v in value))
        codes[z, :, 0:512] = wide[0]
        codes[z, :, 512:768] = thin[0]
        codes[z, :, 768:896] = scales[0]
        return [send(codes.at[z], codes.at[z], at_z(d)) for d in z_order]

    def fold(row):
        return row[:, 0:128] + row[:, 128:256] + row[:, 256:384] + row[:, 384:512]

    def cut(row):
        return [row[:, 128 * i : 128 * (i + 1)] for i in range(4)]

    def uncut(stats, at):
        return jnp.concatenate([stats[at + i : at + i + 1] for i in range(4)], axis=1)

    def plane_start(st, sty, rows):
        value = jnp.concatenate(rows + [jnp.zeros((16 - len(rows), 128), F32)], axis=0)
        st[...] = value
        sty[me] = value
        sends = [send(st, sty.at[me], at_y(d)) for d in (2, 1, 3)]
        sends += [send(st, sty.at[me], at_y(d, True)) for d in (2, 1, 3)]
        return sends + [send(st, sty.at[me], sibling)]

    def plane_finish(sends, sty, sts, stz):
        arrived(sends)
        group = jnp.sum(sty[...], axis=0)
        sts[...] = group
        stz[z] = group
        return [send(sts, stz.at[z], at_z(d)) for d in z_order]

    r3rd = ring(3, r2nd)
    r4th = ring(4, r3rd)
    mine = [p1[i, y] for i in range(3)]
    for d in (1, 3, 2):
        py[d].wait_recv()
        more = unpack(pr1[lax.rem(y + NY - d, NY)])
        mine = [a + b for a, b in zip(mine, more)]
    fill(s1, c1, mine)
    rs1 = scatter_z(c1, r1)
    qy = to_y(qc)

    for d, copy in zip((1, 3, 2), xs):
        copy.wait_recv()
        src = lax.rem(x + NX - d, NX)
        gsib.append(send(grads.at[src, tokens], grads.at[src, tokens], sibling))
    arrived(gsib)
    arrived(r4th.values())
    cot = jnp.zeros((256, 256), F32)
    for i in range(NZ):
        both = jnp.concatenate(
            [grads[j, :, 128 * i : 128 * (i + 1)] for j in range(NX)], axis=1
        )
        cot = cot + dot_nn(both, oall[i])
    rows = pl.ds(2 * y, 2)

    def half(core):
        return pl.ds(pl.multiple_of(core * 256, 256), 256)

    cot_top = row_top(cot)
    oc[rows, :, half(c)] = encode(cot, cot_top).reshape(2, TOK, 256)
    for j in (0, 1):
        otops[c, 2 * y + j] = jnp.broadcast_to(
            as_row(cot_top[TOK * j : TOK * (j + 1)] * STEP), (8, TOK)
        )
    tops_here = otops.at[c, rows]
    here = oc.at[rows, :, half(c)]
    otsends = [send(tops_here, tops_here, at_y(d)) for d in y_order]
    coty = {d: send(here, here, at_y(d)) for d in y_order}
    cot_hi, cot_lo = halves(cot)
    o2[rows, 0, :, half(c)] = cot_hi.reshape(2, TOK, 256)
    o2[rows, 1, :, half(c)] = cot_lo.reshape(2, TOK, 256)
    there = o2.at[rows, :, :, half(c)]
    cotsib = [send(there, there, sibling)]

    pg_c, pu_c, pd_c = summed(s1, r1, rs1)
    ag1 = gather_z(a1, (pg_c, pu_c, pd_c))
    gc, uc, wc = gs[y, z], us[y, z], wts[y, z]
    ys1 = plane_start(
        st1, sty1,
        [fold(col_sum(pg_c * pg_c)), fold(col_sum(pu_c * pu_c))]
        + cut(col_sum(pd_c * pd_c)) + cut(col_sum(wc * pd_c)) + cut(col_sum(wc * wc)),
    )

    zs1 = plane_finish(ys1, sty1, sts1, stz1)
    ky = to_y(kc)
    ty = to_y(tc)

    qsib += open_blocks(q2, qc, qy)
    arrived(otsends)
    for d in y_order:
        coty[d].wait_recv()
        first_block = 2 * lax.rem(y + NY - d, NY)
        for j in (0, 1):
            block = first_block + j
            scale = as_columns(otops[c, block][0:1], 2)
            for i, part in enumerate(halves(decode(oc[block, :, half(c)]) * scale)):
                o2[block, i, :, half(c)] = part
        there = o2.at[pl.ds(first_block, 2), :, :, half(c)]
        cotsib.append(send(there, there, sibling))
    arrived(tsends)
    k_scale, t_scale, q_scale = (scale_row(i) for i in range(3))
    arrived(qsib)
    arrived(cotsib)
    arrived(zs1)
    arrived(ag1)

    with jax.named_scope("renormed"):
        stats = jnp.sum(stz1[...], axis=0)
        d_pp, d_wp, d_ww = uncut(stats, 2), uncut(stats, 6), uncut(stats, 10)
        pn_g = jnp.sqrt(total(stats[0:1]) + EPS)
        pn_u = jnp.sqrt(total(stats[1:2]) + EPS)
        pn_d = jnp.sqrt(total(d_pp) + EPS)
        k_g, k_u, k_d = SCALE / pn_g, SCALE / pn_u, SCALE / pn_d
        old_d = jnp.sqrt(d_ww + EPS)
        new_d = jnp.sqrt(
            jnp.maximum(d_ww - 2.0 * k_d * d_wp + k_d * k_d * d_pp, 0.0) + EPS
        )
        d_pm = d_wp - k_d * d_pp

        def moved_rows(matrix, partial, k):
            moved = matrix - partial * k
            old = jnp.sqrt(row_sum(matrix * matrix) + EPS)
            new = jnp.sqrt(row_sum(moved * moved) + EPS)
            return moved, old, new

        g_m, u_m, w_m = flat(gs), flat(us), flat(wts)
        p_g, p_u, p_d = (v.reshape(FS, D) for v in unpack(a1[...]))
        mv_g, old_g, new_g = moved_rows(g_m, p_g, k_g)
        mv_u, old_u, new_u = moved_rows(u_m, p_u, k_u)
        mv_d = w_m - p_d * k_d
        ren_gu = jnp.concatenate([mv_g * (old_g / new_g), mv_u * (old_u / new_u)], axis=0)
        ren_d = mv_d * (old_d / new_d)

    with jax.named_scope("cotangents"):
        both = q_scale * three(dot_nt, ren_gu, *whole(q2))
        before, linear = both[:FS], both[FS:]
        hcot = three(dot_nt, ren_d, *whole(o2))
        sigma, act, dsilu = silu_parts(before)
        acts_q = jnp.concatenate([hcot * linear * dsilu, hcot * act], axis=0)
        cgu = three(dot_nn, q_scale * acts_q, *whole(q2))
        cd = three(dot_nn, act * linear, *whole(o2))
        fill(s2, c2, [v.reshape(NZ, 8, D) for v in (cgu[:FS], cgu[FS:], cd)])
    rs2 = scatter_z(c2, r2)
    def to_sibling(part, sib):
        copies = {}
        for d in (2, 1, 3, 0):
            to = lax.rem(y + d, NY)
            copies[d] = send(part.at[to, 1 - c], sib.at[to], sibling)
        return copies

    with jax.named_scope("query_grad"):
        part_q[...] = back(acts_q, ren_gu).reshape(NY, 2, TOK, D)
    sibq = to_sibling(part_q, sib_q)
    ksib = open_blocks(k2, kc, ky)
    tsib = open_blocks(t2, tc, ty)

    cg_c, cu_c, cd_c = summed(s2, r2, rs2)
    ag2 = gather_z(a2, (cg_c, cu_c, cd_c))

    def row_back(matrix, partial, k, grad):
        moved, old, new = moved_rows(matrix, partial, k)
        along = row_sum(moved * grad)
        moved_grad = (old / new) * (grad - moved * (along / (new * new)))
        return moved_grad, moved_grad + (along / (new * old)) * matrix

    mg_c, direct_g = row_back(gc, pg_c, k_g, cg_c)
    mu_c, direct_u = row_back(uc, pu_c, k_u, cu_c)
    ys2 = plane_start(
        st2, sty2,
        [fold(-col_sum(pg_c * mg_c)), fold(-col_sum(pu_c * mu_c))]
        + cut(col_sum((wc - pd_c * k_d) * cd_c)) + cut(col_sum(pd_c * cd_c)),
    )

    def to_owner(part, sib, plain, codes, scales, rec, rec_scales, copies):
        sends = {}
        for d in (2, 1, 3):
            to = lax.rem(y + d, NY)
            copies[d].wait_recv()
            value = part[to, c] + sib[to]
            top = row_top(value)
            codes[to] = encode(value, top)
            scales[to] = jnp.broadcast_to(as_row(top * STEP), (8, TOK))
            sends[d] = (
                send(codes.at[to], rec.at[y], at_y(d)),
                send(scales.at[to], rec_scales.at[y], at_y(d)),
            )
        copies[0].wait_recv()
        plain[...] = part[y, c] + sib[y]
        return sends

    def owned(plain, rec, rec_scales, copies):
        value = plain[...]
        for d in (1, 3, 2):
            arrived(copies[d])
            src = lax.rem(y + NY - d, NY)
            value = value + decode(rec[src]) * as_columns(rec_scales[src][0:1], 4)
        return value

    yq = to_owner(part_q, sib_q, sum_q, code_q, ctop_q, rec_q, rtop_q, sibq)
    zs2 = plane_finish(ys2, sty2, sts2, stz2)
    arrived(ksib)
    arrived(tsib)
    with jax.named_scope("key_products"):
        both = k_scale * three(
            dot_nt, jnp.concatenate([flat(gs), flat(us)], axis=0), *whole(k2)
        )
        before_s[...] = both[:FS]
        linear_s[...] = both[FS:]
        hgrad_s[...] = t_scale * three(dot_nt, flat(wts), *whole(t2))

    arrived(zs2)
    arrived(ag2)
    with jax.named_scope("direction"):
        stats2 = jnp.sum(stz2[...], axis=0)
        inner_g, inner_u = total(stats2[0:1]), total(stats2[1:2])
        along_d, d_pg = uncut(stats2, 2), uncut(stats2, 6)
        ratio_d = old_d / new_d
        shrink_d = along_d / (new_d * new_d)
        inner_d = -total(ratio_d * (d_pg - d_pm * shrink_d))
        c_g, c_u, c_d = (v.reshape(FS, D) for v in unpack(a2[...]))
        mgrad_g, _ = row_back(g_m, p_g, k_g, c_g)
        mgrad_u, _ = row_back(u_m, p_u, k_u, c_u)
        mgrad_d = ratio_d * (c_d - mv_d * shrink_d)
        direct_d = mgrad_d + (along_d / (new_d * old_d)) * w_m
        dir_g = -k_g * (mgrad_g + p_g * (inner_g / (pn_g * pn_g)))
        dir_u = -k_u * (mgrad_u + p_u * (inner_u / (pn_u * pn_u)))
        dir_d = -k_d * (mgrad_d + p_d * (inner_d / (pn_d * pn_d)))

    with jax.named_scope("through"):
        both = k_scale * three(dot_nt, jnp.concatenate([dir_g, dir_u], axis=0), *whole(k2))
        d_bg, d_lg = both[:FS], both[FS:]
        d_hid = t_scale * three(dot_nt, dir_d, *whole(t2))
        before, linear, hgrad = before_s[...], linear_s[...], hgrad_s[...]
        sigma, act, dsilu = silu_parts(before)
        curve = sigma * (1.0 - sigma) * (2.0 + before * (1.0 - 2.0 * sigma))
        d_h = d_bg * linear * dsilu + d_lg * act
        d_l = d_bg * hgrad * dsilu + d_hid * act
        d_b = d_bg * hgrad * linear * curve + (d_lg * hgrad + d_hid * linear) * dsilu
        part_t[...] = back(
            jnp.concatenate([act * linear, d_h], axis=0),
            jnp.concatenate([dir_d, w_m], axis=0),
        ).reshape(NY, 2, TOK, D)
        sibt = to_sibling(part_t, sib_t)
        part_k[...] = back(
            jnp.concatenate([hgrad * linear * dsilu, hgrad * act, d_b, d_l], axis=0),
            jnp.concatenate([dir_g, dir_u, g_m, u_m], axis=0),
        ).reshape(NY, 2, TOK, D)
        sibk = to_sibling(part_k, sib_k)
        yt = to_owner(part_t, sib_t, sum_t, code_t, ctop_t, rec_t, rtop_t, sibt)
        th_d = three(dot_nn, t_scale * d_h, *whole(t2))
        th_d = th_d + jnp.where(z == 0, direct_d, jnp.zeros_like(direct_d))
        th_d = th_d.reshape(NZ, 1, 8, D)
        none = jnp.zeros_like(th_d)
        th_d = jnp.concatenate(
            [jnp.where(first, th_d, none), jnp.where(first, none, th_d)], axis=1
        ).reshape(2 * FS, D)
        th_t = th_d.T.reshape(NY, NZ, 2, 8, 2 * FS)
        for i in range(NZ):
            d3[i] = th_t[:, i].reshape(8, 8, 2 * FS)
        rsd = scatter_z(d3, rd3)
        yk = to_owner(part_k, sib_k, sum_k, code_k, ctop_k, rec_k, rtop_k, sibk)
        th_gu = three(dot_nn, k_scale * jnp.concatenate([d_b, d_l], axis=0), *whole(k2))
        th_gu = jnp.concatenate(
            [th_gu[:FS].reshape(NZ, 8, D), th_gu[FS:].reshape(NZ, 8, D)], axis=1
        )
        s3[...] = th_gu
        top_bf = (row_top(th_gu) * 1.01).astype(BF16)
        top = top_bf.astype(F32)
        c3[:, :, 0:512] = encode(th_gu, top)
        c3[:, :, 512:640] = jnp.broadcast_to(top, (NZ, 16, 128)).astype(BF16)
        rs3 = scatter_z(c3, r3)

    qg_ref[...] = owned(sum_q, rec_q, rtop_q, yq)
    down = d3[z]
    for d, copy in zip(z_order, rsd):
        copy.wait_recv()
        down = down + rd3[lax.rem(z + NZ - d, NZ)]
    ds3[...] = down
    dr3[me] = ds3[me]
    fin = [send(ds3.at[2 * y + 1 - c], dr3.at[me], sibling)]
    for d in (1, 2, 3):
        to = 2 * lax.rem(y + d, NY)
        fin.append(send(ds3.at[to + c], dr3.at[me], at_y(d)))
        fin.append(send(ds3.at[to + 1 - c], dr3.at[me], at_y(d, True)))
    vg_ref[...] = -(rate_full * owned(sum_t, rec_t, rtop_t, yt))
    kg_ref[...] = owned(sum_k, rec_k, rtop_k, yk)
    gate_up = s3[z]
    for d, copy in zip(z_order, rs3):
        copy.wait_recv()
        codes = r3[lax.rem(z + NZ - d, NZ)]
        gate_up = gate_up + decode(codes[:, 0:512]) * (
            codes[:, 512:640].astype(F32)[:, 0:1] * STEP
        )
    gg_ref[...] = gate_up[0:8] + direct_g
    ug_ref[...] = gate_up[8:16] + direct_u
    arrived(fin)
    dg_ref[...] = jnp.concatenate(
        [dr3[2 * i] + dr3[2 * i + 1] for i in range(NY)], axis=1
    )
    for copy in started:
        copy.wait_send()


def hand_over(*refs):
    for i in range(6):
        refs[6 + i][...] = refs[i][...]


def body(queries, keys, values, rates, gate_fast, up_fast, down_fast, out_proj, out_grad):
    vmem = pl.BlockSpec(memory_space=pltpu.VMEM)
    hbm = pl.BlockSpec(memory_space=pl.ANY)

    def buf(*shape, dtype=F32):
        return pltpu.VMEM(shape, dtype)

    exchange = [
        buf(3, NZ, 8, D), *[buf(NZ, 16, 896, dtype=BF16)] * 3,
        buf(16, 128), buf(8, 16, 128), buf(16, 128), buf(NZ, 16, 128),
    ]
    grads = [
        buf(NY, 2, TOK, D), buf(NY, TOK, D), buf(TOK, D),
        buf(NY, TOK, D, dtype=BF16), buf(NY, 8, TOK),
        buf(NY, TOK, D, dtype=BF16), buf(NY, 8, TOK),
    ]
    outs = pl.pallas_call(
        kernel,
        out_shape=[jax.ShapeDtypeStruct((TOK, D), F32)] * 3
        + [jax.ShapeDtypeStruct((8, D), F32)] * 3,
        in_specs=[vmem] * 4 + [hbm] * 3 + [vmem] * 2,
        out_specs=[vmem] * 6,
        scratch_shapes=[buf(2, 2, TOK, D, dtype=BF16)] * 2
        + [buf(8, 2, TOK, D, dtype=BF16)] * 4
        + [buf(8, TOK, D, dtype=BF16)] * 4
        + [
            buf(8, TOK), buf(8, 8, TOK), buf(2, 8, 8, TOK),
            buf(64, 256, dtype=BF16),
            buf(NZ, 512, 256, dtype=BF16),
            buf(NX, 256, 1024, dtype=BF16),
            buf(NY, NZ, 8, D), buf(NY, NZ, 8, D), buf(D, D), buf(NY, NZ, 8, D),
        ]
        + [buf(FS, 8 * TOK)] * 3
        + [buf(3, NY, NZ, 8, D), *[buf(NY, NZ, 16, 896, dtype=BF16)] * 2]
        + exchange
        + exchange
        + [
            buf(NZ, 16, D), *[buf(NZ, 16, 640, dtype=BF16)] * 2,
            buf(NZ, 8, 8, 128), buf(NZ, 8, 8, 128), buf(8, 8, 128), buf(8, 8, 128),
        ]
        + grads * 3
        + [pltpu.SemaphoreType.DMA((420,)), pltpu.SemaphoreType.DMA((3,))],
        compiler_params=pltpu.CompilerParams(
            collective_id=0, has_side_effects=True, vmem_limit_bytes=58 * 2**20
        ),
    )(
        queries, keys, values, rates,
        gate_fast.reshape(NY, NZ, 2, 8, D), up_fast.reshape(NY, NZ, 2, 8, D),
        down_fast.reshape(D, D), out_proj.T, out_grad,
    )
    outs = pl.pallas_call(
        hand_over,
        out_shape=[jax.ShapeDtypeStruct(o.shape, F32) for o in outs],
        in_specs=[vmem] * 6,
        out_specs=[vmem] * 6,
    )(*outs)
    return (*outs[:3], *(o.reshape(1, 8, D) for o in outs[3:]))


def solution(mesh):
    torus = Mesh(mesh.devices.reshape(NY, NZ, NC, NX), ("y", "z", "c", "head"))
    return jax.shard_map(
        body,
        mesh=torus,
        in_specs=(
            P(SEQ, "head"), P(SEQ, "head"), P(SEQ, "head"), P("head", SEQ),
            P("head", None, None), P("head", None, None), P("head", None, None),
            P("head", SEQ), P(SEQ, "head"),
        ),
        out_specs=(
            P(SEQ, "head"), P(SEQ, "head"), P(SEQ, "head"),
            P("head", SEQ, None), P("head", SEQ, None), P("head", SEQ, None),
        ),
        check_vma=False,
    )
```

```python
import math

import jax
import jax.numpy as jnp
from jax import lax
from jax.experimental import pallas as pl
from jax.experimental.pallas import tpu as pltpu
from jax.sharding import Mesh
from jax.sharding import PartitionSpec as P

MESH = pl.DeviceIdType.MESH
SEQ = ("y", "z", "c")
F32 = jnp.float32
BF16 = jnp.bfloat16
NY, NZ, NC, NX = 4, 8, 2, 4
TOK = 128
D = 512
FS = 64
SCALE = 0.3 * math.sqrt(512)
EPS = 1e-06
SPAN = 251.0
LOW = 125.0
LN2 = math.log(2.0)
STEP = 1.0 / (SPAN * LN2)


def halves(x):
    hi = x.astype(BF16)
    return hi, (x - hi.astype(F32)).astype(BF16)


def dot_nt(a, b):
    return lax.dot_general(a, b, (((1,), (1,)), ((), ())), preferred_element_type=F32)


def dot_nn(a, b):
    return lax.dot_general(a, b, (((1,), (0,)), ((), ())), preferred_element_type=F32)


def dot_tn(a, b):
    return lax.dot_general(a, b, (((0,), (0,)), ((), ())), preferred_element_type=F32)


def three(product, a, b_hi, b_lo):
    hi, lo = halves(a)
    n = a.shape[0]
    both = product(jnp.concatenate([hi, lo], axis=0), b_hi)
    return both[:n] + both[n:] + product(hi, b_lo)


def back(acts, mats):
    a_hi, a_lo = halves(acts)
    m_hi, m_lo = halves(mats)
    return dot_tn(
        jnp.concatenate([a_hi, a_lo, a_hi], axis=0), jnp.concatenate([m_hi, m_hi, m_lo], axis=0)
    )


def encode(x, top):
    size = jnp.exp(jnp.abs(x) * (SPAN * LN2 / top) - LOW * LN2)
    return jnp.where(x < 0, -size, size).astype(BF16)


def decode(codes):
    value = codes.astype(F32)
    size = jnp.log(jnp.abs(value)) + LOW * LN2
    return jnp.where(value < 0, -size, size)


def row_top(x):
    return jnp.maximum(jnp.max(jnp.abs(x), axis=-1, keepdims=True), 1e-30)


def as_row(column):
    return jnp.broadcast_to(column, (TOK, TOK)).T[0:1]


def as_columns(row, tiles):
    return jnp.concatenate([jnp.broadcast_to(row, (TOK, TOK)).T] * tiles, axis=1)


def pack(gate, up, down):
    wide = jnp.concatenate([gate, up], axis=1)
    thin = jnp.concatenate([down[..., :256], down[..., 256:]], axis=1)
    top_w = (row_top(wide) * 1.01).astype(BF16)
    top_t = (row_top(thin) * 1.01).astype(BF16)
    top_w32, top_t32 = top_w.astype(F32), top_t.astype(F32)
    lanes = (*wide.shape[:2], 64)
    tops = jnp.concatenate(
        [jnp.broadcast_to(top_w32, lanes), jnp.broadcast_to(top_t32, lanes)], axis=2
    ).astype(BF16)
    return encode(wide, top_w32), encode(thin, top_t32), tops


def unpack(codes):
    tops = codes[..., 768:896].astype(F32) * STEP
    wide = decode(codes[..., :512]) * tops[..., 0:1]
    thin = decode(codes[..., 512:768]) * tops[..., 64:65]
    down = jnp.concatenate([thin[:, :8], thin[:, 8:]], axis=2)
    return wide[:, :8], wide[:, 8:], down


def row_sum(x):
    return jnp.sum(x, axis=1, keepdims=True)


def col_sum(x):
    return jnp.sum(x, axis=0, keepdims=True)


def total(x):
    return jnp.sum(jnp.sum(x, axis=1, keepdims=True), axis=0, keepdims=True)


def kernel(
    q_ref, k_ref, v_ref, rate_ref, g_hbm, u_hbm, w_hbm, oproj_ref, ograd_ref,
    qg_ref, kg_ref, vg_ref, gg_ref, ug_ref, dg_ref,
    k1, t1, k2, t2, q2, o2, kc, tc, qc, oc, tops_s, tops, otops, oproj_sib, oall, grads,
    gs, us, wcol, wts,
    before_s, linear_s, hgrad_s,
    p1, pc1, pr1, s1, c1, r1, a1, st1, sty1, sts1, stz1,
    s2, c2, r2, a2, st2, sty2, sts2, stz2,
    s3, c3, r3, d3, rd3, ds3, dr3,
    part_q, sib_q, sum_q, code_q, ctop_q, rec_q, rtop_q,
    part_k, sib_k, sum_k, code_k, ctop_k, rec_k, rtop_k,
    part_t, sib_t, sum_t, code_t, ctop_t, rec_t, rtop_t,
    sems, lsem,
):
    y, z, c, x = (lax.axis_index(name) for name in ("y", "z", "c", "head"))
    used = [0]

    def at_y(dy, other=False):
        return (lax.rem(y + dy, NY), z, 1 - c if other else c, x)

    def at_z(dz):
        return (y, lax.rem(z + dz, NZ), c, x)

    def at_x(dx):
        return (y, z, c, lax.rem(x + dx, NX))

    sibling = (y, z, 1 - c, x)
    y_order = (1, 3, 2)
    z_order = (4, 3, 5, 2, 6, 1, 7)

    def send(src, dst, device):
        i = used[0]
        used[0] += 2
        copy = pltpu.make_async_remote_copy(
            src_ref=src, dst_ref=dst, send_sem=sems.at[i], recv_sem=sems.at[i + 1],
            device_id=device, device_id_type=MESH,
        )
        copy.start()
        started.append(copy)
        return copy

    started = []

    def arrived(copies):
        for copy in copies:
            copy.wait_recv()

    loads = []
    for i, (src, dst) in enumerate(
        (
            (g_hbm.at[:, :, c], gs),
            (u_hbm.at[:, :, c], us),
            (w_hbm, wcol),
        )
    ):
        copy = pltpu.make_async_copy(src, dst, lsem.at[i])
        copy.start()
        loads.append(copy)

    barrier = pltpu.get_barrier_semaphore()
    partners = [sibling]
    partners += [at_y(d) for d in (1, 2, 3)] + [at_y(d, True) for d in (1, 2, 3)]
    partners += [at_z(d) for d in range(1, NZ)] + [at_x(d) for d in (1, 2, 3)]
    for device in partners:
        pl.semaphore_signal(barrier, inc=1, device_id=device, device_id_type=MESH)
    me = 2 * y + c
    first = c == 0
    rate_full = as_columns(rate_ref[...], 4)
    target = -(rate_full * v_ref[...])
    for near, value in ((k1, k_ref[...]), (t1, target)):
        for i, part in enumerate(halves(value)):
            near[c, i] = part
    tokens = pl.ds(pl.multiple_of(c * TOK, TOK), TOK)
    grads[x, tokens, :] = ograd_ref[...]
    for copy in loads:
        copy.wait()
    wt = wcol[...].T.reshape(NY, NZ, 2, 8, D)
    wts[...] = jnp.where(first, wt[:, :, 0], wt[:, :, 1])

    pl.semaphore_wait(barrier, len(partners))

    osib = send(
        oproj_ref.at[:, pl.ds(pl.multiple_of((1 - c) * 256, 256), 256)], oproj_sib, sibling
    )
    near = [send(k1.at[c], k1.at[c], sibling), send(t1.at[c], t1.at[c], sibling)]
    xs = [send(grads.at[x, tokens], grads.at[x, tokens], at_x(d)) for d in (1, 3, 2)]
    gsib = [send(grads.at[x, tokens], grads.at[x, tokens], sibling)]
    def to_y(codes):
        return {d: send(codes.at[me], codes.at[me], at_y(d)) for d in y_order}

    def open_blocks(buffer, codes, copies):
        result = []
        for d in y_order:
            copies[d].wait_recv()
            block = 2 * lax.rem(y + NY - d, NY) + c
            for i, part in enumerate(halves(decode(codes[block]))):
                buffer[block, i] = part
            result.append(send(buffer.at[block], buffer.at[block], sibling))
        return result

    osib.wait_recv()
    own = oproj_ref[:, pl.ds(pl.multiple_of(c * 256, 256), 256)]
    yrows = pl.multiple_of(y * 128, 128)
    oall[z, pl.ds(pl.multiple_of(yrows + c * 64, 64), 64)] = own
    oall[z, pl.ds(pl.multiple_of(yrows + (1 - c) * 64, 64), 64)] = oproj_sib[...]
    ohere = oall.at[z, pl.ds(yrows, 128)]
    oy = [send(ohere, ohere, at_y(d)) for d in y_order]
    def ring(step, previous):
        result = {}
        for half in (0, 1):
            for way in (1, -1):
                if step == 4 and (half == 0) != (way == 1):
                    continue
                if previous is not None:
                    previous[half, way].wait_recv()
                block = lax.rem(z + NZ - way * (step - 1), NZ)
                part = oall.at[block, pl.ds(256 * half, 256)]
                result[half, way] = send(part, part, at_z((way + NZ) % NZ))
        if step == 4:
            for key in ((1, 1), (0, -1)):
                previous[key].wait_recv()
        return result

    def scale_row(i):
        return jnp.concatenate([tops[b, i : i + 1] for b in range(8)], axis=1)

    def flat(ref):
        return ref[y].reshape(FS, D)

    def whole(buffer):
        return tuple(buffer[:, i].reshape(8 * TOK, D) for i in (0, 1))

    def silu_parts(before):
        sigma = jax.nn.sigmoid(before)
        return sigma, before * sigma, sigma * (1.0 + before * (1.0 - sigma))

    arrived(near)
    with jax.named_scope("partials"):
        k_near = tuple(k1[:, i].reshape(2 * TOK, D) for i in (0, 1))
        t_near = tuple(t1[:, i].reshape(2 * TOK, D) for i in (0, 1))
        n = NY * FS
        both = three(
            dot_nt,
            jnp.concatenate([gs[...].reshape(n, D), us[...].reshape(n, D)], axis=0),
            *k_near,
        )
        before, linear = both[:n], both[n:]
        hgrad = three(dot_nt, wts[...].reshape(n, D), *t_near)
    arrived(oy)
    r1st = ring(1, None)
    with jax.named_scope("partials"):
        sigma, act, dsilu = silu_parts(before)
        pgu = three(
            dot_nn, jnp.concatenate([hgrad * linear * dsilu, hgrad * act], axis=0), *k_near
        )
        p1[0] = pgu[:n].reshape(NY, NZ, 8, D)
        p1[1] = pgu[n:].reshape(NY, NZ, 8, D)
        p1[2] = three(dot_nn, act * linear, *t_near).reshape(NY, NZ, 8, D)

    def put(codes, index, values):
        wide, thin, scales = pack(*values)
        codes[index, :, :, 0:512] = wide
        codes[index, :, :, 512:768] = thin
        codes[index, :, :, 768:896] = scales

    py = {}
    for d in (2, 1, 3):
        to = lax.rem(y + d, NY)
        put(pc1, to, tuple(p1[i, to] for i in range(3)))
        py[d] = send(pc1.at[to], pr1.at[y], at_y(d))
    r2nd = ring(2, r1st)

    own_tops = []
    for buffer, near, codes, value in (
        (k2, k1, kc, k_ref[...]), (t2, t1, tc, target), (q2, None, qc, q_ref[...])
    ):
        top = row_top(value)
        codes[me] = encode(value, top)
        own_tops.append(as_row(top * STEP))
        if near is None:
            for i, part in enumerate(halves(value)):
                buffer[me, i] = part
        else:
            buffer[pl.ds(2 * y, 2)] = near[...]
    tops_s[...] = jnp.concatenate(own_tops + [jnp.zeros((5, TOK), F32)], axis=0)
    tops[pl.ds(2 * y, 2)] = jnp.ones((2, 8, TOK), F32)
    tsends = [send(tops_s, tops.at[me], at_y(d)) for d in (1, 2, 3)]
    tsends += [send(tops_s, tops.at[me], at_y(d, True)) for d in (1, 2, 3)]
    qsib = [send(q2.at[me], q2.at[me], sibling)]

    def fill(plain, codes, parts):
        for i in range(3):
            plain[i] = parts[i]
        wide, thin, scales = pack(*parts)
        codes[:, :, 0:512] = wide
        codes[:, :, 512:768] = thin
        codes[:, :, 768:896] = scales

    def scatter_z(src, dst):
        return [
            send(src.at[lax.rem(z + d, NZ)], dst.at[z], at_z(d)) for d in z_order
        ]

    def summed(plain, dst, copies):
        value = [plain[i, z] for i in range(3)]
        for d, copy in zip(z_order, copies):
            copy.wait_recv()
            more = unpack(dst[pl.ds(lax.rem(z + NZ - d, NZ), 1)])
            value = [a + b[0] for a, b in zip(value, more)]
        return value

    def gather_z(codes, value):
        wide, thin, scales = pack(*(v[None] for v in value))
        codes[z, :, 0:512] = wide[0]
        codes[z, :, 512:768] = thin[0]
        codes[z, :, 768:896] = scales[0]
        return [send(codes.at[z], codes.at[z], at_z(d)) for d in z_order]

    def fold(row):
        return row[:, 0:128] + row[:, 128:256] + row[:, 256:384] + row[:, 384:512]

    def cut(row):
        return [row[:, 128 * i : 128 * (i + 1)] for i in range(4)]

    def uncut(stats, at):
        return jnp.concatenate([stats[at + i : at + i + 1] for i in range(4)], axis=1)

    def plane_start(st, sty, rows):
        value = jnp.concatenate(rows + [jnp.zeros((16 - len(rows), 128), F32)], axis=0)
        st[...] = value
        sty[me] = value
        sends = [send(st, sty.at[me], at_y(d)) for d in (2, 1, 3)]
        sends += [send(st, sty.at[me], at_y(d, True)) for d in (2, 1, 3)]
        return sends + [send(st, sty.at[me], sibling)]

    def plane_finish(sends, sty, sts, stz):
        arrived(sends)
        group = jnp.sum(sty[...], axis=0)
        sts[...] = group
        stz[z] = group
        return [send(sts, stz.at[z], at_z(d)) for d in z_order]

    r3rd = ring(3, r2nd)
    mine = [p1[i, y] for i in range(3)]
    for d in (1, 3, 2):
        py[d].wait_recv()
        more = unpack(pr1[lax.rem(y + NY - d, NY)])
        mine = [a + b for a, b in zip(mine, more)]
    fill(s1, c1, mine)
    r4th = ring(4, r3rd)
    rs1 = scatter_z(c1, r1)
    qy = to_y(qc)

    for d, copy in zip((1, 3, 2), xs):
        copy.wait_recv()
        src = lax.rem(x + NX - d, NX)
        gsib.append(send(grads.at[src, tokens], grads.at[src, tokens], sibling))
    arrived(gsib)
    arrived(r4th.values())
    cot = jnp.zeros((256, 256), F32)
    for i in range(NZ):
        both = jnp.concatenate(
            [grads[j, :, 128 * i : 128 * (i + 1)] for j in range(NX)], axis=1
        )
        cot = cot + dot_nn(both, oall[i])
    rows = pl.ds(2 * y, 2)

    def half(core):
        return pl.ds(pl.multiple_of(core * 256, 256), 256)

    cot_top = row_top(cot)
    oc[rows, :, half(c)] = encode(cot, cot_top).reshape(2, TOK, 256)
    for j in (0, 1):
        otops[c, 2 * y + j] = jnp.broadcast_to(
            as_row(cot_top[TOK * j : TOK * (j + 1)] * STEP), (8, TOK)
        )
    tops_here = otops.at[c, rows]
    here = oc.at[rows, :, half(c)]
    otsends = [send(tops_here, tops_here, at_y(d)) for d in y_order]
    coty = {d: send(here, here, at_y(d)) for d in y_order}
    cot_hi, cot_lo = halves(cot)
    o2[rows, 0, :, half(c)] = cot_hi.reshape(2, TOK, 256)
    o2[rows, 1, :, half(c)] = cot_lo.reshape(2, TOK, 256)
    there = o2.at[rows, :, :, half(c)]
    cotsib = [send(there, there, sibling)]

    pg_c, pu_c, pd_c = summed(s1, r1, rs1)
    ag1 = gather_z(a1, (pg_c, pu_c, pd_c))
    gc, uc, wc = gs[y, z], us[y, z], wts[y, z]
    ys1 = plane_start(
        st1, sty1,
        [fold(col_sum(pg_c * pg_c)), fold(col_sum(pu_c * pu_c))]
        + cut(col_sum(pd_c * pd_c)) + cut(col_sum(wc * pd_c)) + cut(col_sum(wc * wc)),
    )

    zs1 = plane_finish(ys1, sty1, sts1, stz1)
    ky = to_y(kc)
    ty = to_y(tc)

    qsib += open_blocks(q2, qc, qy)
    arrived(otsends)
    for d in y_order:
        coty[d].wait_recv()
        first_block = 2 * lax.rem(y + NY - d, NY)
        for j in (0, 1):
            block = first_block + j
            scale = as_columns(otops[c, block][0:1], 2)
            for i, part in enumerate(halves(decode(oc[block, :, half(c)]) * scale)):
                o2[block, i, :, half(c)] = part
        there = o2.at[pl.ds(first_block, 2), :, :, half(c)]
        cotsib.append(send(there, there, sibling))
    arrived(tsends)
    k_scale, t_scale, q_scale = (scale_row(i) for i in range(3))
    arrived(qsib)
    arrived(cotsib)
    arrived(zs1)
    arrived(ag1)

    with jax.named_scope("renormed"):
        stats = jnp.sum(stz1[...], axis=0)
        d_pp, d_wp, d_ww = uncut(stats, 2), uncut(stats, 6), uncut(stats, 10)
        pn_g = jnp.sqrt(total(stats[0:1]) + EPS)
        pn_u = jnp.sqrt(total(stats[1:2]) + EPS)
        pn_d = jnp.sqrt(total(d_pp) + EPS)
        k_g, k_u, k_d = SCALE / pn_g, SCALE / pn_u, SCALE / pn_d
        old_d = jnp.sqrt(d_ww + EPS)
        new_d = jnp.sqrt(
            jnp.maximum(d_ww - 2.0 * k_d * d_wp + k_d * k_d * d_pp, 0.0) + EPS
        )
        d_pm = d_wp - k_d * d_pp

        def moved_rows(matrix, partial, k):
            moved = matrix - partial * k
            old = jnp.sqrt(row_sum(matrix * matrix) + EPS)
            new = jnp.sqrt(row_sum(moved * moved) + EPS)
            return moved, old, new

        g_m, u_m, w_m = flat(gs), flat(us), flat(wts)
        p_g, p_u, p_d = (v.reshape(FS, D) for v in unpack(a1[...]))
        mv_g, old_g, new_g = moved_rows(g_m, p_g, k_g)
        mv_u, old_u, new_u = moved_rows(u_m, p_u, k_u)
        mv_d = w_m - p_d * k_d
        ren_gu = jnp.concatenate([mv_g * (old_g / new_g), mv_u * (old_u / new_u)], axis=0)
        ren_d = mv_d * (old_d / new_d)

    with jax.named_scope("cotangents"):
        both = q_scale * three(dot_nt, ren_gu, *whole(q2))
        before, linear = both[:FS], both[FS:]
        hcot = three(dot_nt, ren_d, *whole(o2))
        sigma, act, dsilu = silu_parts(before)
        acts_q = jnp.concatenate([hcot * linear * dsilu, hcot * act], axis=0)
        cgu = three(dot_nn, q_scale * acts_q, *whole(q2))
        cd = three(dot_nn, act * linear, *whole(o2))
        fill(s2, c2, [v.reshape(NZ, 8, D) for v in (cgu[:FS], cgu[FS:], cd)])
    rs2 = scatter_z(c2, r2)
    def to_sibling(part, sib):
        copies = {}
        for d in (2, 1, 3, 0):
            to = lax.rem(y + d, NY)
            copies[d] = send(part.at[to, 1 - c], sib.at[to], sibling)
        return copies

    with jax.named_scope("query_grad"):
        part_q[...] = back(acts_q, ren_gu).reshape(NY, 2, TOK, D)
    sibq = to_sibling(part_q, sib_q)
    ksib = open_blocks(k2, kc, ky)
    tsib = open_blocks(t2, tc, ty)

    cg_c, cu_c, cd_c = summed(s2, r2, rs2)
    ag2 = gather_z(a2, (cg_c, cu_c, cd_c))

    def row_back(matrix, partial, k, grad):
        moved, old, new = moved_rows(matrix, partial, k)
        along = row_sum(moved * grad)
        moved_grad = (old / new) * (grad - moved * (along / (new * new)))
        return moved_grad, moved_grad + (along / (new * old)) * matrix

    mg_c, direct_g = row_back(gc, pg_c, k_g, cg_c)
    mu_c, direct_u = row_back(uc, pu_c, k_u, cu_c)
    ys2 = plane_start(
        st2, sty2,
        [fold(-col_sum(pg_c * mg_c)), fold(-col_sum(pu_c * mu_c))]
        + cut(col_sum((wc - pd_c * k_d) * cd_c)) + cut(col_sum(pd_c * cd_c)),
    )

    def to_owner(part, sib, plain, codes, scales, rec, rec_scales, copies):
        sends = {}
        for d in (2, 1, 3):
            to = lax.rem(y + d, NY)
            copies[d].wait_recv()
            value = part[to, c] + sib[to]
            top = row_top(value)
            codes[to] = encode(value, top)
            scales[to] = jnp.broadcast_to(as_row(top * STEP), (8, TOK))
            sends[d] = (
                send(codes.at[to], rec.at[y], at_y(d)),
                send(scales.at[to], rec_scales.at[y], at_y(d)),
            )
        copies[0].wait_recv()
        plain[...] = part[y, c] + sib[y]
        return sends

    def owned(plain, rec, rec_scales, copies):
        value = plain[...]
        for d in (1, 3, 2):
            arrived(copies[d])
            src = lax.rem(y + NY - d, NY)
            value = value + decode(rec[src]) * as_columns(rec_scales[src][0:1], 4)
        return value

    yq = to_owner(part_q, sib_q, sum_q, code_q, ctop_q, rec_q, rtop_q, sibq)
    zs2 = plane_finish(ys2, sty2, sts2, stz2)
    arrived(ksib)
    arrived(tsib)
    with jax.named_scope("key_products"):
        both = k_scale * three(
            dot_nt, jnp.concatenate([flat(gs), flat(us)], axis=0), *whole(k2)
        )
        before_s[...] = both[:FS]
        linear_s[...] = both[FS:]
        hgrad_s[...] = t_scale * three(dot_nt, flat(wts), *whole(t2))
        before, linear, hgrad = before_s[...], linear_s[...], hgrad_s[...]
        sigma, act, dsilu = silu_parts(before)
        curve = sigma * (1.0 - sigma) * (2.0 + before * (1.0 - 2.0 * sigma))
        hidden, before_grad, linear_grad = act * linear, hgrad * linear * dsilu, hgrad * act

    arrived(zs2)
    arrived(ag2)
    with jax.named_scope("direction"):
        stats2 = jnp.sum(stz2[...], axis=0)
        inner_g, inner_u = total(stats2[0:1]), total(stats2[1:2])
        along_d, d_pg = uncut(stats2, 2), uncut(stats2, 6)
        ratio_d = old_d / new_d
        shrink_d = along_d / (new_d * new_d)
        inner_d = -total(ratio_d * (d_pg - d_pm * shrink_d))
        c_g, c_u, c_d = (v.reshape(FS, D) for v in unpack(a2[...]))
        mgrad_g, _ = row_back(g_m, p_g, k_g, c_g)
        mgrad_u, _ = row_back(u_m, p_u, k_u, c_u)
        mgrad_d = ratio_d * (c_d - mv_d * shrink_d)
        direct_d = mgrad_d + (along_d / (new_d * old_d)) * w_m
        dir_g = -k_g * (mgrad_g + p_g * (inner_g / (pn_g * pn_g)))
        dir_u = -k_u * (mgrad_u + p_u * (inner_u / (pn_u * pn_u)))
        dir_d = -k_d * (mgrad_d + p_d * (inner_d / (pn_d * pn_d)))

    with jax.named_scope("through"):
        both = k_scale * three(dot_nt, jnp.concatenate([dir_g, dir_u], axis=0), *whole(k2))
        d_bg, d_lg = both[:FS], both[FS:]
        d_hid = t_scale * three(dot_nt, dir_d, *whole(t2))
        d_h = d_bg * linear * dsilu + d_lg * act
        d_l = d_bg * hgrad * dsilu + d_hid * act
        d_b = d_bg * hgrad * linear * curve + (d_lg * hgrad + d_hid * linear) * dsilu
        part_t[...] = back(
            jnp.concatenate([hidden, d_h], axis=0),
            jnp.concatenate([dir_d, w_m], axis=0),
        ).reshape(NY, 2, TOK, D)
        sibt = to_sibling(part_t, sib_t)
        part_k[...] = back(
            jnp.concatenate([before_grad, linear_grad, d_b, d_l], axis=0),
            jnp.concatenate([dir_g, dir_u, g_m, u_m], axis=0),
        ).reshape(NY, 2, TOK, D)
        sibk = to_sibling(part_k, sib_k)
        yt = to_owner(part_t, sib_t, sum_t, code_t, ctop_t, rec_t, rtop_t, sibt)
        th_d = three(dot_nn, t_scale * d_h, *whole(t2))
        th_d = th_d + jnp.where(z == 0, direct_d, jnp.zeros_like(direct_d))
        th_d = th_d.reshape(NZ, 1, 8, D)
        none = jnp.zeros_like(th_d)
        th_d = jnp.concatenate(
            [jnp.where(first, th_d, none), jnp.where(first, none, th_d)], axis=1
        ).reshape(2 * FS, D)
        th_t = th_d.T.reshape(NY, NZ, 2, 8, 2 * FS)
        for i in range(NZ):
            d3[i] = th_t[:, i].reshape(8, 8, 2 * FS)
        rsd = scatter_z(d3, rd3)
        yk = to_owner(part_k, sib_k, sum_k, code_k, ctop_k, rec_k, rtop_k, sibk)
        th_gu = three(dot_nn, k_scale * jnp.concatenate([d_b, d_l], axis=0), *whole(k2))
        th_gu = jnp.concatenate(
            [th_gu[:FS].reshape(NZ, 8, D), th_gu[FS:].reshape(NZ, 8, D)], axis=1
        )
        s3[...] = th_gu
        top_bf = (row_top(th_gu) * 1.01).astype(BF16)
        top = top_bf.astype(F32)
        c3[:, :, 0:512] = encode(th_gu, top)
        c3[:, :, 512:640] = jnp.broadcast_to(top, (NZ, 16, 128)).astype(BF16)
        rs3 = scatter_z(c3, r3)

    qg_ref[...] = owned(sum_q, rec_q, rtop_q, yq)
    down = d3[z]
    for d, copy in zip(z_order, rsd):
        copy.wait_recv()
        down = down + rd3[lax.rem(z + NZ - d, NZ)]
    ds3[...] = down
    dr3[me] = ds3[me]
    fin = [send(ds3.at[2 * y + 1 - c], dr3.at[me], sibling)]
    for d in (1, 2, 3):
        to = 2 * lax.rem(y + d, NY)
        fin.append(send(ds3.at[to + c], dr3.at[me], at_y(d)))
        fin.append(send(ds3.at[to + 1 - c], dr3.at[me], at_y(d, True)))
    vg_ref[...] = -(rate_full * owned(sum_t, rec_t, rtop_t, yt))
    kg_ref[...] = owned(sum_k, rec_k, rtop_k, yk)
    gate_up = s3[z]
    for d, copy in zip(z_order, rs3):
        copy.wait_recv()
        codes = r3[lax.rem(z + NZ - d, NZ)]
        gate_up = gate_up + decode(codes[:, 0:512]) * (
            codes[:, 512:640].astype(F32)[:, 0:1] * STEP
        )
    gg_ref[...] = gate_up[0:8] + direct_g
    ug_ref[...] = gate_up[8:16] + direct_u
    arrived(fin)
    dg_ref[...] = jnp.concatenate(
        [dr3[2 * i] + dr3[2 * i + 1] for i in range(NY)], axis=1
    )
    for copy in started:
        copy.wait_send()


def hand_over(*refs):
    for i in range(6):
        refs[6 + i][...] = refs[i][...]


def body(queries, keys, values, rates, gate_fast, up_fast, down_fast, out_proj, out_grad):
    vmem = pl.BlockSpec(memory_space=pltpu.VMEM)
    hbm = pl.BlockSpec(memory_space=pl.ANY)

    def buf(*shape, dtype=F32):
        return pltpu.VMEM(shape, dtype)

    exchange = [
        buf(3, NZ, 8, D), *[buf(NZ, 16, 896, dtype=BF16)] * 3,
        buf(16, 128), buf(8, 16, 128), buf(16, 128), buf(NZ, 16, 128),
    ]
    grads = [
        buf(NY, 2, TOK, D), buf(NY, TOK, D), buf(TOK, D),
        buf(NY, TOK, D, dtype=BF16), buf(NY, 8, TOK),
        buf(NY, TOK, D, dtype=BF16), buf(NY, 8, TOK),
    ]
    outs = pl.pallas_call(
        kernel,
        out_shape=[jax.ShapeDtypeStruct((TOK, D), F32)] * 3
        + [jax.ShapeDtypeStruct((8, D), F32)] * 3,
        in_specs=[vmem] * 4 + [hbm] * 3 + [vmem] * 2,
        out_specs=[vmem] * 6,
        scratch_shapes=[buf(2, 2, TOK, D, dtype=BF16)] * 2
        + [buf(8, 2, TOK, D, dtype=BF16)] * 4
        + [buf(8, TOK, D, dtype=BF16)] * 4
        + [
            buf(8, TOK), buf(8, 8, TOK), buf(2, 8, 8, TOK),
            buf(64, 256, dtype=BF16),
            buf(NZ, 512, 256, dtype=BF16),
            buf(NX, 256, 1024, dtype=BF16),
            buf(NY, NZ, 8, D), buf(NY, NZ, 8, D), buf(D, D), buf(NY, NZ, 8, D),
        ]
        + [buf(FS, 8 * TOK)] * 3
        + [buf(3, NY, NZ, 8, D), *[buf(NY, NZ, 16, 896, dtype=BF16)] * 2]
        + exchange
        + exchange
        + [
            buf(NZ, 16, D), *[buf(NZ, 16, 640, dtype=BF16)] * 2,
            buf(NZ, 8, 8, 128), buf(NZ, 8, 8, 128), buf(8, 8, 128), buf(8, 8, 128),
        ]
        + grads * 3
        + [pltpu.SemaphoreType.DMA((420,)), pltpu.SemaphoreType.DMA((3,))],
        compiler_params=pltpu.CompilerParams(
            collective_id=0, has_side_effects=True, vmem_limit_bytes=58 * 2**20
        ),
    )(
        queries, keys, values, rates,
        gate_fast.reshape(NY, NZ, 2, 8, D), up_fast.reshape(NY, NZ, 2, 8, D),
        down_fast.reshape(D, D), out_proj.T, out_grad,
    )
    outs = pl.pallas_call(
        hand_over,
        out_shape=[jax.ShapeDtypeStruct(o.shape, F32) for o in outs],
        in_specs=[vmem] * 6,
        out_specs=[vmem] * 6,
    )(*outs)
    return (*outs[:3], *(o.reshape(1, 8, D) for o in outs[3:]))


def solution(mesh):
    torus = Mesh(mesh.devices.reshape(NY, NZ, NC, NX), ("y", "z", "c", "head"))
    return jax.shard_map(
        body,
        mesh=torus,
        in_specs=(
            P(SEQ, "head"), P(SEQ, "head"), P(SEQ, "head"), P("head", SEQ),
            P("head", None, None), P("head", None, None), P("head", None, None),
            P("head", SEQ), P(SEQ, "head"),
        ),
        out_specs=(
            P(SEQ, "head"), P(SEQ, "head"), P(SEQ, "head"),
            P("head", SEQ, None), P("head", SEQ, None), P("head", SEQ, None),
        ),
        check_vma=False,
    )
```
